32 devices in a mesh: tp: 4 (over y, x), rows: 8 (over z, core).
Axes of the slice: x: 2, y: 2, z: 4, core: 2. Of those that a mesh axis runs over, the one named last changes fastest.
Arguments:
- block_input: bfloat16 [4096, 1024], P('rows', 'tp'), may hold values from -6 to 6
- first_gain: float32 [1024], replicated, may hold values from 0.5 to 1.5
- first_shift: float32 [1024], replicated, may hold values from -3 to 3
- qkv_weight: bfloat16 [3, 1024, 1024], P(None, None, 'tp'), may hold values from -0.1875 to 0.1875
- qv_bias: float32 [2, 1024], P(None, 'tp'), may hold values from -3 to 3
- out_weight: bfloat16 [1024, 1024], P('tp'), may hold values from -1.5 to 1.5
- out_bias: float32 [1024], P('tp'), may hold values from -3 to 3
- second_gain: float32 [1024], replicated, may hold values from 0.5 to 1.5
- second_shift: float32 [1024], replicated, may hold values from -3 to 3
- up_weight: bfloat16 [1024, 4096], P(None, 'tp'), may hold values from -0.1875 to 0.1875
- up_bias: float32 [4096], P('tp'), may hold values from -3 to 3
- down_weight: bfloat16 [4096, 1024], P('tp'), may hold values from -0.1875 to 0.1875
- down_bias: float32 [1024], P('tp'), may hold values from -3 to 3
- memory_keys: bfloat16 [163840, 1024], P('rows', 'tp'), may hold values from -6 to 6
- memory_ids: int32 [4096, 64], P('rows'), may hold values from 0 to 163839, as said below
- doc_lengths: int32 [8, 3], P('rows'), may hold values from 1 to 256, 512 in all within a row
- out_cotangent: bfloat16 [4096, 1024], P('rows', 'tp'), may hold values from -6 to 6
- score_cotangent: bfloat16 [4096, 64], P('rows'), may hold values from -6 to 6
Outputs:
- block_output: bfloat16 [4096, 1024], P('rows', 'tp')
- memory_scores: float32 [4096, 64], P('rows')
- input_grad: float32 [4096, 1024], P('rows', 'tp')
- first_gain_grad: float32 [1024], P('tp')
- first_shift_grad: float32 [1024], P('tp')
- qkv_grad: float32 [3, 1024, 1024], P(None, 'rows', 'tp')
- qv_bias_grad: float32 [2, 1024], P(None, 'tp')
- out_weight_grad: float32 [1024, 1024], P('tp', 'rows')
- out_bias_grad: float32 [1024], P('tp')
- second_gain_grad: float32 [1024], P('tp')
- second_shift_grad: float32 [1024], P('tp')
- up_weight_grad: float32 [1024, 4096], P('rows', 'tp')
- up_bias_grad: float32 [4096], P('tp')
- down_weight_grad: float32 [4096, 1024], P('tp', 'rows')
- down_bias_grad: float32 [1024], P('tp')
- memory_grad: float32 [163840, 1024], P('rows', 'tp')
The draws below stay inside these ranges and needn't reach their ends.
Inputs may be any that keep to these rules, and one draw needn't show every extreme that they name: `memory_ids`: entry r is stored on the index r // 20480 of rows. Of the 32768 ids of one device, at most 6144 name entries stored on any one index, and one index, the same for every device of a draw, is named exactly 6144 times by each device.
All inputs are finite; a program needn't handle non-finite values.
Results may differ from the reference program's by a relative error of at most 0.012.
Values may be sent and summed in bfloat16 or wider, within the bound.
A program may use at most 320 MiB of HBM per device.

```python
import math
import jax
import jax.numpy as jnp
import numpy as np
from jax import lax

D = 1024
HEADS = 16
HD = 64
FF = 4096
K = 64
SEGS = 3
MEMORY = 163840
TOK_DEV = 512
SEG_MOST = 256
SHARDS = 8
TOKENS = 4096
N_ROWS = 8


def draw_memory_ids(key, part):
    key = jax.random.fold_in(key, 7)
    requests = TOK_DEV * K
    share = requests // N_ROWS
    owner_rows = MEMORY // N_ROWS
    hot_key, rest_key = jax.random.split(key)
    hot_owner = jax.random.randint(hot_key, (), 0, N_ROWS)

    def one_device(device_key):
        split_keys = jax.random.split(device_key, 5)
        owner_order = jax.random.permutation(split_keys[0], N_ROWS)
        leading = owner_order[0]
        positions = jnp.arange(N_ROWS)
        owner_order = jnp.where(positions == 0, hot_owner, jnp.where(owner_order == hot_owner, leading, owner_order))
        excess = jax.random.randint(split_keys[1], (N_ROWS // 2,), 0, share // 2 + 1)
        excess = jnp.where(jnp.arange(N_ROWS // 2) == 0, share // 2, excess)
        counts = jnp.zeros((N_ROWS,), jnp.int32)
        counts = counts.at[owner_order[0::2]].set(share + excess)
        counts = counts.at[owner_order[1::2]].set(share - excess)
        bounds = jnp.cumsum(counts)
        places = jnp.arange(requests)
        owners = jnp.searchsorted(bounds, places, side='right').astype(jnp.int32)
        owners = owners[jax.random.permutation(split_keys[2], requests)]
        uniform_rows = jax.random.randint(split_keys[3], (requests,), 0, owner_rows)
        skewed = uniform_rows * uniform_rows // owner_rows
        offsets = jax.random.randint(split_keys[4], (N_ROWS,), 0, owner_rows)
        local_rows = (skewed + offsets[owners]) % owner_rows
        return (owners * owner_rows + local_rows).reshape(TOK_DEV, K)
    identifiers = jax.vmap(one_device)(jax.random.split(rest_key, N_ROWS))
    return identifiers.reshape(TOK_DEV * N_ROWS, K).astype(jnp.int32)


def steps_of(own_key, shape, cuts, low, largest):
    def one(position, shards_of):
        steps = jax.random.uniform(jax.random.fold_in(jax.random.fold_in(own_key, 6), position), (shards_of,), jnp.float32, low / len(cuts), largest / len(cuts))
        return jnp.repeat(jnp.exp(steps), shape[position] // shards_of).reshape((-1,) + (1,) * (len(shape) - position - 1))

    loudness = one(*cuts[0])
    for cut in cuts[1:]:
        loudness = loudness * one(*cut)
    return loudness


def length_profile(count, total, reach, slope):
    weights = [(1 << 20) // math.isqrt(standing ** slope) + 1 for standing in range(2, count + 1)]
    surplus, holding = total - reach - (count - 1), [1] * (count - 1)
    while surplus > 0:
        movable = [i for i in range(count - 1) if holding[i] < reach]
        pool, left = sum([weights[i] for i in movable]), surplus
        for i in movable:
            more = min(reach - holding[i], max(1, left * weights[i] // pool), surplus)
            holding[i] = holding[i] + more
            surplus = surplus - more
    return np.array([reach] + holding)


def uneven(rng, number_of, total, limit, skew):
    if number_of == 2:
        one = jax.random.randint(rng, (), max(1, total - limit), min(limit, total - 1) + 1)
        return jnp.stack([one, total - one])
    tallies = jnp.asarray(length_profile(number_of, total, limit, skew), jnp.int32)
    twos = (number_of - 1) // 2
    giver, receiver = tallies[1:1 + 2 * twos:2], tallies[2:2 + 2 * twos:2]
    room = jnp.minimum(giver - 1, limit - receiver)
    moved = jax.random.randint(jax.random.fold_in(rng, 1), (twos,), 0, 1 << 20) % (room + 1)
    tallies = tallies.at[1:1 + 2 * twos:2].set(giver - moved).at[2:2 + 2 * twos:2].set(receiver + moved)
    return tallies[jax.random.permutation(jax.random.fold_in(rng, 2), number_of)]


def scatter_about(stream_key, shape, width, bound, pieces=(), kind=jnp.bfloat16):
    entries = width * jax.random.normal(stream_key, shape, jnp.float32)
    if pieces:
        entries = entries * steps_of(stream_key, shape, pieces, -0.22, 0.18)
    return jnp.clip(entries, -bound, bound).astype(kind)


def setup_inputs(seed: int = 0) -> dict:
    key_list = jax.random.split(jax.random.key(seed), 19)
    block_input = scatter_about(key_list[0], (TOKENS, D), 1.0, 6.0, ((0, 8), (1, 4)))
    first_gain = jnp.clip(1.0 + 0.1 * jax.random.normal(key_list[1], (D,), jnp.float32), 0.5, 1.5)
    first_shift = scatter_about(key_list[2], (D,), 0.5, 3.0, (), jnp.float32)
    qkv_weight = scatter_about(key_list[3], (3, D, D), D ** -0.5, 0.1875, ((2, 4),))
    qv_bias = scatter_about(key_list[4], (2, D), 0.5, 3.0, ((1, 4),), jnp.float32)
    out_weight = scatter_about(key_list[5], (D, D), 16 ** -0.5, 1.5, ((0, 4),))
    out_bias = scatter_about(key_list[6], (D,), 0.5, 3.0, ((0, 4),), jnp.float32)
    second_gain = jnp.clip(1.0 + 0.1 * jax.random.normal(key_list[7], (D,), jnp.float32), 0.5, 1.5)
    second_shift = scatter_about(key_list[8], (D,), 0.5, 3.0, (), jnp.float32)
    up_weight = scatter_about(key_list[9], (D, FF), D ** -0.5, 0.1875, ((1, 4),))
    up_bias = scatter_about(key_list[10], (FF,), 0.5, 3.0, ((0, 4),), jnp.float32)
    down_weight = scatter_about(key_list[11], (FF, D), (FF // 4) ** -0.5, 0.1875, ((0, 4),))
    down_bias = scatter_about(key_list[12], (D,), 0.5, 3.0, ((0, 4),), jnp.float32)
    memory_keys = scatter_about(key_list[13], (MEMORY, D), 1.0, 6.0, ((0, 8), (1, 4)))
    memory_ids = draw_memory_ids(jax.random.fold_in(key_list[18], 71), 0)
    doc_lengths = jax.vmap(lambda own: uneven(own, SEGS, TOK_DEV, SEG_MOST, 1))(jax.random.split(key_list[15], SHARDS)).reshape((SHARDS, SEGS)).astype(jnp.int32)
    out_cotangent = scatter_about(key_list[16], (TOKENS, D), 1.0, 6.0, ((0, 8), (1, 4)))
    score_cotangent = scatter_about(key_list[17], (TOKENS, K), 1.0, 6.0, ((0, 8),))
    return {"block_input": block_input, "first_gain": first_gain, "first_shift": first_shift, "qkv_weight": qkv_weight, "qv_bias": qv_bias, "out_weight": out_weight, "out_bias": out_bias, "second_gain": second_gain, "second_shift": second_shift, "up_weight": up_weight, "up_bias": up_bias, "down_weight": down_weight, "down_bias": down_bias, "memory_keys": memory_keys, "memory_ids": memory_ids, "doc_lengths": doc_lengths, "out_cotangent": out_cotangent, "score_cotangent": score_cotangent}


@jax.custom_vjp
def low(v):
    return lax.optimization_barrier(v.astype(jnp.bfloat16)).astype(jnp.float32)

@jax.custom_vjp
def low_back(v):
    return v

def low_keep(v):
    return (low(v), None)

def low_pass(kept, grad):
    return (grad,)

def back_keep(v):
    return (v, None)

def back_low(kept, grad):
    return (low(grad),)
low.defvjp(low_keep, low_pass)
low_back.defvjp(back_keep, back_low)
exact_mode = lax.Precision.HIGHEST

def matmul(left, right):
    return jnp.dot(left, right, precision=exact_mode)

def layer_norm(values, gain, shift):
    row_mean = lax.optimization_barrier(jnp.mean(values, axis=1, keepdims=True))
    centered = values - row_mean
    row_var = lax.optimization_barrier(jnp.mean(centered * centered, axis=1, keepdims=True))
    return centered * lax.rsqrt(row_var + 1e-05) * gain + shift

def segment_of(lengths, row_count):
    places = jnp.arange(row_count, dtype=jnp.int32)
    bounds = jnp.cumsum(lengths).astype(jnp.int32)
    segment = lax.optimization_barrier(jnp.sum((places[:, None] >= bounds[None, :]).astype(jnp.int32), axis=1))
    return (segment, places)

def block_forward(params, memory, tokens, lengths, retrieved):
    first_gain, first_shift, qkv_weight, qv_bias, out_weight, out_bias, second_gain, second_shift, up_weight, up_bias, down_weight, down_bias = params
    row_count = tokens.shape[0]
    normed = low(layer_norm(tokens, first_gain, first_shift))
    queries = low_back(low(matmul(normed, qkv_weight[0]) + qv_bias[0])).reshape(row_count, HEADS, HD)
    key_rows = low_back(low(matmul(normed, qkv_weight[1]))).reshape(row_count, HEADS, HD)
    values = low_back(low(matmul(normed, qkv_weight[2]) + qv_bias[1])).reshape(row_count, HEADS, HD)
    segment, places = segment_of(lengths, row_count)
    allowed = (segment[:, None] == segment[None, :]) & (places[None, :] <= places[:, None])
    logits = jnp.einsum('qhd,khd->hqk', queries, key_rows, precision=exact_mode) * (1.0 / math.sqrt(HD))
    logits = low_back(jnp.where(allowed[None], logits, -1000000000.0))
    row_peak = lax.optimization_barrier(jnp.max(logits, axis=2, keepdims=True))
    weights = jnp.exp(logits - row_peak)
    attention = low(weights / lax.optimization_barrier(jnp.sum(weights, axis=2, keepdims=True)))
    mixed_heads = jnp.einsum('hqk,khd->qhd', attention, values, precision=exact_mode)
    mixed_heads = low_back(low(mixed_heads)).reshape(row_count, D)
    residual_mid = tokens + low_back(matmul(mixed_heads, out_weight) + out_bias)
    normed_second = low(layer_norm(residual_mid, second_gain, second_shift))
    before = low_back(matmul(normed_second, up_weight) + up_bias)
    active = low(jax.nn.gelu(before, approximate=True))
    result = low(residual_mid + low_back(matmul(active, down_weight) + down_bias))
    fetched = jnp.take(memory, retrieved, axis=0)
    scores = jnp.einsum('tkd,td->tk', fetched, result, precision=exact_mode) * (1.0 / math.sqrt(D))
    return (result, scores)

def reference(block_input, first_gain, first_shift, qkv_weight, qv_bias, out_weight, out_bias, second_gain, second_shift, up_weight, up_bias, down_weight, down_bias, memory_keys, memory_ids, doc_lengths, out_cotangent, score_cotangent):
    params = tuple((item.astype(jnp.float32) for item in (first_gain, first_shift, qkv_weight, qv_bias, out_weight, out_bias, second_gain, second_shift, up_weight, up_bias, down_weight, down_bias)))
    memory = memory_keys.astype(jnp.float32)

    def full_forward(tokens, weights_all, table):

        def single(items):
            return block_forward(weights_all, table, items[0], items[1], items[2])
        results, scores = lax.map(jax.checkpoint(single), (tokens.reshape(SHARDS, TOK_DEV, D), doc_lengths, memory_ids.reshape(SHARDS, TOK_DEV, K)))
        return (results.reshape(TOKENS, D), scores.reshape(TOKENS, K))
    (results, scores), pullback = jax.vjp(full_forward, block_input.astype(jnp.float32), params, memory)
    input_grad, grads, memory_grad = pullback((out_cotangent.astype(jnp.float32), score_cotangent.astype(jnp.float32)))
    return (results.astype(jnp.bfloat16), scores, input_grad, grads[0], grads[1], grads[2], grads[3], grads[4], grads[5], grads[6], grads[7], grads[8], grads[9], grads[10], grads[11], memory_grad)
```

```python
import functools
import math

import jax
import jax.numpy as jnp
from jax import lax
from jax.experimental import pallas as pl
from jax.experimental.pallas import tpu as pltpu
from jax.sharding import PartitionSpec as P

HD = 64
CHUNK = 256
WINDOW = 512
CHAINS = 5
NT = (((1,), (1,)), ((), ()))


def log2(size):
    return size.bit_length() - 1


def one_hot(row, size, value=None):
    one = jnp.ones((1, row.shape[1]), jnp.bfloat16) if value is None else value.astype(jnp.bfloat16)
    place = lax.broadcasted_iota(jnp.int32, (256, row.shape[1]), 0).astype(jnp.bfloat16)
    parts = []
    for k in range(size // 256):
        near = jnp.clip(row - 256 * k, -1, 256).astype(jnp.bfloat16)
        parts.append(jnp.where(place == near, one, jnp.zeros((), jnp.bfloat16)))
    return parts[0] if len(parts) == 1 else jnp.concatenate(parts, axis=0)


def spans_of(span_ref, first, n):
    lows = [span_ref[(first + k) * 2] for k in range(n)]
    counts = [span_ref[(first + k) * 2 + 1] - lows[k] for k in range(n)]
    return lows, functools.reduce(jnp.maximum, counts)


def fetch_kernel(span_ref, packed_ref, weight_ref, keys_ref, found_ref, grad_ref, acc_ref, *, groups, chains, retrieved):
    src = pl.program_id(0)
    tokens = grad_ref.shape[1]
    window = keys_ref.shape[2]
    last = keys_ref.shape[0] - 1
    grad_ref[0] = jnp.zeros(grad_ref.shape[1:], jnp.float32)

    def group(g, _):
        lows, count = spans_of(span_ref, (src * groups + g) * chains, chains)

        @pl.when(count > 0)
        def _():
            packed = packed_ref[0, pl.ds(g, 1), :]
            entry = packed >> log2(tokens * retrieved)
            token = (packed >> log2(retrieved)) & (tokens - 1)
            entries = [entry[:, k * CHUNK : (k + 1) * CHUNK] for k in range(chains)]

            def product(k, i):
                b = lows[k] + i
                hot = one_hot(entries[k] - b * window, window)
                return jnp.dot(keys_ref[jnp.minimum(b, last)], hot, preferred_element_type=jnp.float32)

            for k in range(chains):
                acc_ref[k] = product(k, 0)

            def step(i, _):
                for k in range(chains):
                    acc_ref[k] += product(k, i)
                return 0

            lax.fori_loop(1, count, step, 0)
            found = jnp.concatenate([acc_ref[k].astype(jnp.bfloat16) for k in range(chains)], axis=1)
            found_ref[0, g] = found
            spread = one_hot(token, tokens, weight_ref[0, pl.ds(g, 1), :])
            grad_ref[0] += lax.dot_general(spread, found, NT, preferred_element_type=jnp.float32)

        return 0

    lax.fori_loop(0, groups, group, 0)


def fetch(span, packed, weight, keys_t, tokens, retrieved, chains):
    n_src, groups, wide = packed.shape
    n_win, width, window = keys_t.shape
    return pl.pallas_call(
        functools.partial(fetch_kernel, groups=groups, chains=chains, retrieved=retrieved),
        grid_spec=pltpu.PrefetchScalarGridSpec(
            num_scalar_prefetch=1,
            grid=(n_src,),
            in_specs=[
                pl.BlockSpec((1, groups, wide), lambda s, *_: (s, 0, 0)),
                pl.BlockSpec((1, groups, wide), lambda s, *_: (s, 0, 0)),
                pl.BlockSpec((n_win, width, window), lambda s, *_: (0, 0, 0)),
            ],
            out_specs=[
                pl.BlockSpec((1, groups, width, wide), lambda s, *_: (s, 0, 0, 0)),
                pl.BlockSpec((1, tokens, width), lambda s, *_: (s, 0, 0)),
            ],
            scratch_shapes=[pltpu.VMEM((chains, width, CHUNK), jnp.float32)],
        ),
        out_shape=[
            jax.ShapeDtypeStruct((n_src, groups, width, wide), jnp.bfloat16),
            jax.ShapeDtypeStruct((n_src, tokens, width), jnp.float32),
        ],
        compiler_params=pltpu.CompilerParams(vmem_limit_bytes=60 * 2**20),
        cost_estimate=pl.CostEstimate(flops=80 * 10**9, bytes_accessed=60 * 10**6, transcendentals=0),
        name="fetch",
    )(span, packed, weight, keys_t)


def spread_kernel(
    span_ref, packed_ref, weight_ref, found_ref, rows_ref, score_ref, mem_ref, *, groups, chains, retrieved, window
):
    src = pl.program_id(0)
    tokens = rows_ref.shape[2]
    last = mem_ref.shape[0] // window - 1

    @pl.when(src == 0)
    def _():
        def zero(b, _):
            mem_ref[pl.ds(pl.multiple_of(b * 256, 256), 256), :] = jnp.zeros((256, mem_ref.shape[1]), jnp.float32)
            return 0

        lax.fori_loop(0, mem_ref.shape[0] // 256, zero, 0)

    score_ref[0] = jnp.zeros(score_ref.shape[1:], jnp.float32)

    def group(g, _):
        lows, count = spans_of(span_ref, (src * groups + g) * chains, chains)

        @pl.when(count > 0)
        def _():
            packed = packed_ref[0, pl.ds(g, 1), :]
            weight = weight_ref[0, pl.ds(g, 1), :]
            entry = packed >> log2(tokens * retrieved)
            token = (packed >> log2(retrieved)) & (tokens - 1)
            column = packed & (retrieved - 1)
            pick = one_hot(token, tokens)
            rows_wide = jnp.dot(rows_ref[0], pick, preferred_element_type=jnp.float32)
            rows = rows_wide.astype(jnp.bfloat16)
            score = jnp.sum(found_ref[0, g].astype(jnp.float32) * rows_wide, axis=0, keepdims=True)
            high_part = score.astype(jnp.bfloat16).astype(jnp.float32)
            low_part = score - high_part
            at = lax.broadcasted_iota(jnp.int32, (retrieved, chains * CHUNK), 0) == column
            columns = jnp.concatenate(
                [jnp.where(at, high_part, 0.0), jnp.where(at, low_part, 0.0)], axis=0
            ).astype(jnp.bfloat16)
            score_ref[0] += lax.dot_general(pick, columns, NT, preferred_element_type=jnp.float32)

            def step(i, _):
                parts = []
                for k in range(chains):
                    part_of = slice(k * CHUNK, (k + 1) * CHUNK)
                    b = lows[k] + i
                    hot = one_hot(entry[:, part_of] - b * window, window, weight[:, part_of])
                    part = lax.dot_general(hot, rows[:, part_of], NT, preferred_element_type=jnp.float32)
                    parts.append((jnp.minimum(b, last), part))
                for b, part in parts:
                    mem_ref[pl.ds(pl.multiple_of(b * window, window), window), :] += part
                return 0

            lax.fori_loop(0, count, step, 0)

        return 0

    lax.fori_loop(0, groups, group, 0)


def spread(span, packed, weight, found, rows_t, entries, retrieved, chains):
    n_src, groups, wide = packed.shape
    _, width, tokens = rows_t.shape
    return pl.pallas_call(
        functools.partial(spread_kernel, groups=groups, chains=chains, retrieved=retrieved, window=WINDOW),
        grid_spec=pltpu.PrefetchScalarGridSpec(
            num_scalar_prefetch=1,
            grid=(n_src,),
            in_specs=[
                pl.BlockSpec((1, groups, wide), lambda s, *_: (s, 0, 0)),
                pl.BlockSpec((1, groups, wide), lambda s, *_: (s, 0, 0)),
                pl.BlockSpec((1, groups, width, wide), lambda s, *_: (s, 0, 0, 0)),
                pl.BlockSpec((1, width, tokens), lambda s, *_: (s, 0, 0)),
            ],
            out_specs=[
                pl.BlockSpec((1, tokens, 2 * retrieved), lambda s, *_: (s, 0, 0)),
                pl.BlockSpec((entries, width), lambda s, *_: (0, 0)),
            ],
        ),
        out_shape=[
            jax.ShapeDtypeStruct((n_src, tokens, 2 * retrieved), jnp.float32),
            jax.ShapeDtypeStruct((entries, width), jnp.float32),
        ],
        compiler_params=pltpu.CompilerParams(vmem_limit_bytes=60 * 2**20),
        cost_estimate=pl.CostEstimate(flops=100 * 10**9, bytes_accessed=60 * 10**6, transcendentals=0),
        name="spread",
    )(span, packed, weight, found, rows_t)


def request_lists(memory_ids, score_cotangent, scale, owner_rows, shards):
    tokens, retrieved = memory_ids.shape
    requests = tokens * retrieved
    capacity = 3 * requests // (2 * shards)
    chunks = -(-(capacity + CHUNK - 1) // CHUNK)
    chains = min(CHAINS, chunks)
    groups = -(-chunks // chains)
    chunks = groups * chains
    flat = memory_ids.reshape(-1)
    place = jnp.arange(requests, dtype=jnp.int32)
    weight = score_cotangent.reshape(-1).astype(jnp.float32) * scale
    ids, place, weight = lax.sort((flat, place, weight), num_keys=1, is_stable=False)
    bounds = jnp.arange(shards, dtype=jnp.int32) * owner_rows
    starts = jnp.sum((flat[None, :] < bounds[:, None]).astype(jnp.int32), axis=1) // CHUNK
    pad = ((0, chunks), (0, 0))
    ids = jnp.pad(ids.reshape(-1, CHUNK), pad, constant_values=-1)
    place = jnp.pad(place.reshape(-1, CHUNK), pad)
    weight = jnp.pad(weight.reshape(-1, CHUNK), pad)
    packed_rows, weight_rows = [], []
    for owner in range(shards):
        own = lax.dynamic_slice_in_dim(ids, starts[owner], chunks, 0) - owner * owner_rows
        own_place = lax.dynamic_slice_in_dim(place, starts[owner], chunks, 0)
        inside = (own >= 0) & (own < owner_rows)
        packed_rows.append(jnp.where(inside, own * requests + own_place, -requests))
        weight_rows.append(lax.dynamic_slice_in_dim(weight, starts[owner], chunks, 0))
    packed = lax.all_to_all(jnp.stack(packed_rows), "rows", split_axis=0, concat_axis=0, tiled=True)
    weight = lax.all_to_all(jnp.stack(weight_rows), "rows", split_axis=0, concat_axis=0, tiled=True)
    entry = packed >> log2(requests)
    low = jnp.min(jnp.where(entry >= 0, entry, owner_rows), axis=2) // WINDOW
    high = jnp.max(entry, axis=2) // WINDOW + 1
    span = jnp.stack([low, high], axis=2).reshape(-1)
    shape = (shards, groups, chains * CHUNK)
    return span, packed.reshape(shape), weight.reshape(shape), chains


def normalize(values):
    row_mean = jnp.mean(values, axis=1, keepdims=True)
    centered = values - row_mean
    row_var = jnp.mean(centered * centered, axis=1, keepdims=True)
    inv_std = lax.rsqrt(row_var + 1e-05)
    return (centered * inv_std, inv_std)


def segment_of(lengths, row_count):
    places = jnp.arange(row_count, dtype=jnp.int32)
    bounds = jnp.cumsum(lengths)
    segment = jnp.sum((places[:, None] >= bounds[None, :]).astype(jnp.int32), axis=1)
    return (segment, places)


def on_device(
    block_input,
    first_gain,
    first_shift,
    qkv_weight,
    qv_bias,
    out_weight,
    out_bias,
    second_gain,
    second_shift,
    up_weight,
    up_bias,
    down_weight,
    down_bias,
    memory_keys,
    memory_ids,
    doc_lengths,
    out_cotangent,
    score_cotangent,
):
    row_count, width = block_input.shape
    full_width = out_weight.shape[1]
    heads = width // HD
    shards = lax.axis_size("rows")
    parts = lax.axis_size("tp")
    retrieved = memory_ids.shape[1]
    owner_rows = memory_keys.shape[0]
    part = lax.axis_index("tp")
    offset = part * width
    own_tokens = row_count // parts
    token_offset = part * own_tokens
    head_scale = 1.0 / math.sqrt(HD)
    memory_scale = 1.0 / math.sqrt(full_width)

    def own_columns(values):
        return lax.dynamic_slice_in_dim(values, offset, width, values.ndim - 1)

    def own_rows(values):
        return lax.dynamic_slice_in_dim(values, token_offset, own_tokens, 0)

    def add_columns(whole, own):
        return lax.dynamic_update_slice_in_dim(whole, own_columns(whole) + own, offset, 1)

    span, packed, weight, chains = request_lists(memory_ids, score_cotangent, memory_scale, owner_rows, shards)
    keys_t = memory_keys.reshape(owner_rows // WINDOW, WINDOW, width).transpose(0, 2, 1)
    found, grad_parts = fetch(span, packed, weight, keys_t, row_count, retrieved, chains)
    memory_part = lax.psum_scatter(grad_parts.reshape(-1, width), "rows", scatter_dimension=0, tiled=True)
    grad_out = out_cotangent.astype(jnp.float32) + memory_part
    down_low = grad_out.astype(jnp.bfloat16)
    full_down = lax.all_gather(down_low, "tp", axis=1, tiled=True)

    inputs_full = lax.all_gather(block_input, "tp", axis=1, tiled=True).astype(jnp.float32)
    normed_first, inv_first = normalize(inputs_full)
    normed_low = (normed_first * first_gain + first_shift).astype(jnp.bfloat16)
    projected = jnp.einsum("td,cde->cte", normed_low, qkv_weight, preferred_element_type=jnp.float32)
    query_heads = (projected[0] + qv_bias[0]).astype(jnp.bfloat16).reshape(row_count, heads, HD)
    key_heads = projected[1].astype(jnp.bfloat16).reshape(row_count, heads, HD)
    value_heads = (projected[2] + qv_bias[1]).astype(jnp.bfloat16).reshape(row_count, heads, HD)
    segment, places = segment_of(doc_lengths[0], row_count)
    allowed = (segment[:, None] == segment[None, :]) & (places[None, :] <= places[:, None])
    logits = jnp.einsum("qhd,khd->hqk", query_heads, key_heads, preferred_element_type=jnp.float32) * head_scale
    logits = jnp.where(allowed[None], logits, -1000000000.0)
    row_peak = jnp.max(logits, axis=2, keepdims=True)
    weights = jnp.exp(logits - row_peak)
    attention = weights / jnp.sum(weights, axis=2, keepdims=True)
    attention_low = attention.astype(jnp.bfloat16)
    mixed_heads = (
        jnp.einsum("hqk,khd->qhd", attention_low, value_heads, preferred_element_type=jnp.float32)
        .astype(jnp.bfloat16)
        .reshape(row_count, width)
    )
    attention_part = jnp.dot(mixed_heads, out_weight, preferred_element_type=jnp.float32)
    attention_part = add_columns(attention_part, block_input.astype(jnp.float32) + out_bias)
    residual_mid = lax.psum_scatter(attention_part, "tp", scatter_dimension=0, tiled=True)
    normed_second, inv_second = normalize(residual_mid)
    second_own = (normed_second * second_gain + second_shift).astype(jnp.bfloat16)
    second_low = lax.all_gather(second_own, "tp", axis=0, tiled=True)
    before = jnp.dot(second_low, up_weight, preferred_element_type=jnp.float32) + up_bias
    gelu_value, gelu_pull = jax.vjp(functools.partial(jax.nn.gelu, approximate=True), before)
    active = gelu_value.astype(jnp.bfloat16)
    down_part = jnp.dot(active, down_weight, preferred_element_type=jnp.float32)
    down_part = add_columns(down_part, down_bias)
    down_part = lax.dynamic_update_slice_in_dim(
        down_part, own_rows(down_part) + residual_mid, token_offset, 0
    )
    output_low = lax.psum_scatter(down_part, "tp", scatter_dimension=1, tiled=True).astype(jnp.bfloat16)

    rows_t = lax.all_gather(output_low.T, "rows", axis=0, tiled=False)
    score_parts, memory_grad = spread(span, packed, weight, found, rows_t, owner_rows, retrieved, chains)
    score_parts = score_parts[:, :, :retrieved] + score_parts[:, :, retrieved:]
    score_own = lax.psum_scatter(score_parts.reshape(-1, retrieved), "rows", scatter_dimension=0, tiled=True)
    memory_scores = lax.psum(score_own, "tp") * memory_scale

    down_bias_grad = jnp.sum(down_low.astype(jnp.float32), axis=0)
    down_weight_grad = jnp.einsum("tf,td->fd", active, full_down, preferred_element_type=jnp.float32)
    active_grad = jnp.einsum("td,fd->tf", full_down, down_weight, preferred_element_type=jnp.float32)
    before_grad = gelu_pull(active_grad)[0].astype(jnp.bfloat16)
    up_bias_grad = jnp.sum(before_grad.astype(jnp.float32), axis=0)
    up_weight_grad = jnp.einsum("td,tf->df", second_low, before_grad, preferred_element_type=jnp.float32)
    second_part = jnp.einsum("tf,df->td", before_grad, up_weight, preferred_element_type=jnp.float32)
    second_grad = lax.psum_scatter(second_part, "tp", scatter_dimension=0, tiled=True)
    scaled = second_grad * second_gain
    row_first = jnp.mean(scaled, axis=1, keepdims=True)
    row_second = jnp.mean(scaled * normed_second, axis=1, keepdims=True)
    mid_own = own_rows(full_down).astype(jnp.float32) + inv_second * (scaled - row_first - normed_second * row_second)
    second_norm_grads = jnp.stack([jnp.sum(second_grad * normed_second, axis=0), jnp.sum(second_grad, axis=0)])
    full_mid = lax.all_gather(mid_own.astype(jnp.bfloat16), "tp", axis=0, tiled=True)
    mid_columns = own_columns(full_mid).astype(jnp.float32)
    out_bias_grad = jnp.sum(mid_columns, axis=0)
    out_weight_grad = jnp.einsum("te,td->ed", mixed_heads, full_mid, preferred_element_type=jnp.float32)
    mixed_grad = (
        jnp.einsum("td,ed->te", full_mid, out_weight, preferred_element_type=jnp.float32)
        .astype(jnp.bfloat16)
        .reshape(row_count, heads, HD)
    )
    grad_attention = jnp.einsum("qhd,khd->hqk", mixed_grad, value_heads, preferred_element_type=jnp.float32)
    row_delta = jnp.sum(attention * grad_attention, axis=2, keepdims=True)
    logit_grad = (attention * (grad_attention - row_delta)).astype(jnp.bfloat16)
    query_grad = jnp.einsum("hqk,khd->qhd", logit_grad, key_heads, preferred_element_type=jnp.float32) * head_scale
    key_grad = jnp.einsum("hqk,qhd->khd", logit_grad, query_heads, preferred_element_type=jnp.float32) * head_scale
    value_grad = jnp.einsum("hqk,qhd->khd", attention_low, mixed_grad, preferred_element_type=jnp.float32)
    stacked = jnp.stack(
        [item.astype(jnp.bfloat16).reshape(row_count, width) for item in (query_grad, key_grad, value_grad)]
    )
    qkv_part = jnp.einsum("td,cte->cde", normed_low, stacked, preferred_element_type=jnp.float32)
    qv_part = jnp.stack([jnp.sum(stacked[c].astype(jnp.float32), axis=0) for c in (0, 2)])
    first_part = jnp.einsum("cte,cde->td", stacked, qkv_weight, preferred_element_type=jnp.float32)
    first_scaled = first_part * first_gain
    row_parts = jnp.stack([jnp.sum(first_scaled, axis=1), jnp.sum(first_scaled * normed_first, axis=1)])
    row_sums = lax.psum(row_parts, "tp") / full_width
    first_grad = lax.psum_scatter(first_part, "tp", scatter_dimension=1, tiled=True)
    normed_own = own_columns(normed_first)
    scaled = first_grad * own_columns(first_gain)
    input_grad = mid_columns + inv_first * (scaled - row_sums[0][:, None] - normed_own * row_sums[1][:, None])
    first_gain_grad = jnp.sum(first_grad * normed_own, axis=0)
    first_shift_grad = jnp.sum(first_grad, axis=0)

    qkv_grad = lax.psum_scatter(qkv_part, "rows", scatter_dimension=1, tiled=True)
    out_weight_total = lax.psum_scatter(out_weight_grad, "rows", scatter_dimension=1, tiled=True)
    up_weight_total = lax.psum_scatter(up_weight_grad, "rows", scatter_dimension=0, tiled=True)
    down_weight_total = lax.psum_scatter(down_weight_grad, "rows", scatter_dimension=1, tiled=True)
    second_norm_total = own_columns(lax.psum(second_norm_grads, ("rows", "tp")))
    small_totals = lax.psum(
        (qv_part, out_bias_grad, up_bias_grad, down_bias_grad, first_gain_grad, first_shift_grad), "rows"
    )
    return (
        output_low,
        memory_scores,
        input_grad,
        small_totals[4],
        small_totals[5],
        qkv_grad,
        small_totals[0],
        out_weight_total,
        small_totals[1],
        second_norm_total[0],
        second_norm_total[1],
        up_weight_total,
        small_totals[2],
        down_weight_total,
        small_totals[3],
        memory_grad,
    )


def solution(mesh):
    return jax.shard_map(
        on_device,
        mesh=mesh,
        in_specs=(
            P("rows", "tp"),
            P(),
            P(),
            P(None, None, "tp"),
            P(None, "tp"),
            P("tp", None),
            P("tp"),
            P(),
            P(),
            P(None, "tp"),
            P("tp"),
            P("tp", None),
            P("tp"),
            P("rows", "tp"),
            P("rows", None),
            P("rows", None),
            P("rows", "tp"),
            P("rows", None),
        ),
        out_specs=(
            P("rows", "tp"),
            P("rows", None),
            P("rows", "tp"),
            P("tp"),
            P("tp"),
            P(None, "rows", "tp"),
            P(None, "tp"),
            P("tp", "rows"),
            P("tp"),
            P("tp"),
            P("tp"),
            P("rows", "tp"),
            P("tp"),
            P("tp", "rows"),
            P("tp"),
            P("rows", "tp"),
        ),
        check_vma=False,
    )
```

```python
import functools
import math

import jax
import jax.numpy as jnp
from jax import lax
from jax.experimental import pallas as pl
from jax.experimental.pallas import tpu as pltpu
from jax.sharding import PartitionSpec as P

HD = 64
CHUNK = 256
WINDOW = 256
CHAINS = 5
PAIRS = 13
LANES = 128
HALVES = CHUNK // LANES
PARTS = 4
MESH = pl.DeviceIdType.MESH
NT = (((1,), (1,)), ((), ()))
TN = (((0,), (0,)), ((), ()))
LIMIT = 60 * 2**20


def log2(size):
    return size.bit_length() - 1


def one_hot(row, size, value=None):
    one = jnp.ones((1, row.shape[1]), jnp.bfloat16) if value is None else value.astype(jnp.bfloat16)
    place = lax.broadcasted_iota(jnp.int32, (256, row.shape[1]), 0).astype(jnp.bfloat16)
    parts = []
    for k in range(size // 256):
        near = jnp.clip(row - 256 * k, -1, 256).astype(jnp.bfloat16)
        parts.append(jnp.where(place == near, one, jnp.zeros((), jnp.bfloat16)))
    return parts[0] if len(parts) == 1 else jnp.concatenate(parts, axis=0)


def pairs_at(pair_ref, src, step):
    pairs = [pair_ref[src, step * PAIRS + k] for k in range(PAIRS)]
    return [(pair >> 8, pair & 255) for pair in pairs]


def chunk_of(ref, c):
    return jnp.concatenate([ref[0, pl.ds(c * HALVES + k, 1), :] for k in range(HALVES)], axis=1)


def chunk_rows(ref, g, chains):
    return jnp.concatenate([chunk_of(ref, g * chains + k) for k in range(chains)], axis=1)


def fetch_kernel(
    pair_ref, count_ref, used_ref, order_ref, packed_ref, weight_ref, keys_ref, found_ref, grad_ref, acc_ref, sum_ref,
    *, chains, retrieved
):
    src = order_ref[pl.program_id(0)]
    tokens = grad_ref.shape[1]
    last = keys_ref.shape[0] // WINDOW - 1
    groups = (used_ref[src] + chains - 1) // chains
    sum_ref[...] = jnp.zeros(sum_ref.shape, jnp.float32)

    def clear(c, _):
        acc_ref[c] = jnp.zeros(acc_ref.shape[1:], jnp.float32)
        return 0

    lax.fori_loop(0, groups * chains, clear, 0)

    def step(i, _):
        parts = []
        for c, b in pairs_at(pair_ref, src, i):
            entry = chunk_of(packed_ref, c) >> log2(tokens * retrieved)
            keys = keys_ref[pl.ds(pl.multiple_of(jnp.minimum(b, last) * WINDOW, WINDOW), WINDOW), :]
            hot = one_hot(entry - b * WINDOW, WINDOW)
            parts.append((c, lax.dot_general(keys, hot, TN, preferred_element_type=jnp.float32)))
        for c, part in parts:
            acc_ref[c] += part
        return 0

    lax.fori_loop(0, (count_ref[src] + PAIRS - 1) // PAIRS, step, 0)

    def group(g, _):
        found = jnp.concatenate([acc_ref[g * chains + k].astype(jnp.bfloat16) for k in range(chains)], axis=1)
        found_ref[0, g] = found
        token = chunk_rows(packed_ref, g, chains) & (tokens - 1)
        spread = one_hot(token, tokens, chunk_rows(weight_ref, g, chains))
        sum_ref[...] += lax.dot_general(spread, found, NT, preferred_element_type=jnp.float32)
        return 0

    lax.fori_loop(0, groups, group, 0)
    grad_ref[0] = sum_ref[...].astype(grad_ref.dtype)


def fetch(table, order, packed, weight, keys, tokens, retrieved, chains):
    n_src = order.shape[0]
    halves = packed.shape[1]
    chunks = halves // HALVES
    entries, width = keys.shape
    lists = pl.BlockSpec((1, halves, LANES), lambda s, pairs, counts, used, order: (order[s], 0, 0))
    return pl.pallas_call(
        functools.partial(fetch_kernel, chains=chains, retrieved=retrieved),
        grid_spec=pltpu.PrefetchScalarGridSpec(
            num_scalar_prefetch=4,
            grid=(n_src,),
            in_specs=[lists, lists, pl.BlockSpec((entries, width), lambda s, *_: (0, 0))],
            out_specs=[
                pl.BlockSpec((1, chunks // chains, width, chains * CHUNK), lambda s, *_: (s, 0, 0, 0)),
                pl.BlockSpec((1, tokens, width), lambda s, *_: (s, 0, 0)),
            ],
            scratch_shapes=[
                pltpu.VMEM((chunks, width, CHUNK), jnp.float32),
                pltpu.VMEM((tokens, width), jnp.float32),
            ],
        ),
        out_shape=[
            jax.ShapeDtypeStruct((n_src, chunks // chains, width, chains * CHUNK), jnp.bfloat16),
            jax.ShapeDtypeStruct((n_src, tokens, width), jnp.bfloat16),
        ],
        compiler_params=pltpu.CompilerParams(vmem_limit_bytes=LIMIT),
        cost_estimate=pl.CostEstimate(flops=10**10 * n_src, bytes_accessed=5 * 10**6 * n_src, transcendentals=0),
        name="fetch",
    )(*table, order, packed, weight, keys)


def score_kernel(used_ref, order_ref, packed_ref, found_ref, rows_ref, score_ref, wide_ref, acc_ref, *, chains, retrieved):
    src = order_ref[pl.program_id(0)]
    tokens = rows_ref.shape[1]
    acc_ref[...] = jnp.zeros(acc_ref.shape, jnp.float32)

    def group(g, _):
        packed = chunk_rows(packed_ref, g, chains)
        token = packed & (tokens - 1)
        column = (packed >> log2(tokens)) & (retrieved - 1)
        pick = one_hot(token, tokens)
        wide = lax.dot_general(rows_ref[0], pick, TN, preferred_element_type=jnp.float32)
        for k in range(chains):
            wide_ref[0, g * chains + k] = wide[:, k * CHUNK : (k + 1) * CHUNK].astype(jnp.bfloat16)
        score = jnp.sum(found_ref[0, g].astype(jnp.float32) * wide, axis=0, keepdims=True)
        high = score.astype(jnp.bfloat16).astype(jnp.float32)
        at = lax.broadcasted_iota(jnp.int32, (retrieved, chains * CHUNK), 0) == column
        columns = jnp.concatenate([jnp.where(at, high, 0.0), jnp.where(at, score - high, 0.0)], axis=0)
        acc_ref[...] += lax.dot_general(columns.astype(jnp.bfloat16), pick, NT, preferred_element_type=jnp.float32)
        return 0

    lax.fori_loop(0, (used_ref[src] + chains - 1) // chains, group, 0)
    score_ref[0] = acc_ref[:retrieved, :] + acc_ref[retrieved:, :]


def score(table, order, packed, found, rows, retrieved, chains):
    n_src = order.shape[0]
    halves = packed.shape[1]
    chunks = halves // HALVES
    _, tokens, width = rows.shape
    return pl.pallas_call(
        functools.partial(score_kernel, chains=chains, retrieved=retrieved),
        grid_spec=pltpu.PrefetchScalarGridSpec(
            num_scalar_prefetch=2,
            grid=(n_src,),
            in_specs=[
                pl.BlockSpec((1, halves, LANES), lambda s, used, order: (order[s], 0, 0)),
                pl.BlockSpec((1, chunks // chains, width, chains * CHUNK), lambda s, *_: (s, 0, 0, 0)),
                pl.BlockSpec((1, tokens, width), lambda s, *_: (s, 0, 0)),
            ],
            out_specs=[
                pl.BlockSpec((1, retrieved, tokens), lambda s, *_: (s, 0, 0)),
                pl.BlockSpec((1, chunks, width, CHUNK), lambda s, *_: (s, 0, 0, 0)),
            ],
            scratch_shapes=[pltpu.VMEM((2 * retrieved, tokens), jnp.float32)],
        ),
        out_shape=[
            jax.ShapeDtypeStruct((n_src, retrieved, tokens), jnp.float32),
            jax.ShapeDtypeStruct((n_src, chunks, width, CHUNK), jnp.bfloat16),
        ],
        compiler_params=pltpu.CompilerParams(vmem_limit_bytes=LIMIT),
        cost_estimate=pl.CostEstimate(flops=5 * 10**9 * n_src, bytes_accessed=5 * 10**6 * n_src, transcendentals=0),
        name="score",
    )(table[2], order, packed, found, rows)


def spread_kernel(pair_ref, count_ref, order_ref, packed_ref, weight_ref, *refs, shift, part, sources):
    wide_refs, mem_ref = refs[:sources], refs[-1]
    each = pl.num_programs(0) // sources
    src = order_ref[pl.program_id(0)]
    windows = mem_ref.shape[0] // WINDOW

    def window(b):
        return pl.ds(pl.multiple_of(jnp.clip(b - part * windows, 0, windows - 1) * WINDOW, WINDOW), WINDOW)

    @pl.when(pl.program_id(0) == 0)
    def _():
        def clear(b, _):
            mem_ref[pl.ds(pl.multiple_of(b * WINDOW, WINDOW), WINDOW), :] = jnp.zeros((WINDOW, mem_ref.shape[1]), jnp.float32)
            return 0

        lax.fori_loop(0, windows, clear, 0)

    def step(wide_ref, i, _):
        parts = []
        for c, b in pairs_at(pair_ref, src, i):
            entry = chunk_of(packed_ref, c) >> shift
            hot = one_hot(entry - b * WINDOW, WINDOW, chunk_of(weight_ref, c))
            parts.append((b, lax.dot_general(hot, wide_ref[0, c], NT, preferred_element_type=jnp.float32)))
        for b, term in parts:
            mem_ref[window(b), :] += term
        return 0

    for n, wide_ref in enumerate(wide_refs):

        @pl.when(pl.program_id(0) // each == n)
        def _(wide_ref=wide_ref):
            lax.fori_loop(0, (count_ref[src] + PAIRS - 1) // PAIRS, functools.partial(step, wide_ref), 0)


def spread(tables, order, packed, weight, wide_rows, entries, shift, part, partly):
    n_src, halves, _ = packed.shape
    chunks = halves // HALVES
    width = wide_rows[0].shape[2]
    each = n_src // len(wide_rows)
    pairs, counts = (table[part] for table in tables)
    parts = tables[0].shape[0]
    lists = pl.BlockSpec((1, halves, LANES), lambda s, pairs, counts, order: (order[s], 0, 0))
    before = [] if partly is None else [partly]
    return pl.pallas_call(
        functools.partial(spread_kernel, shift=shift, part=part, sources=len(wide_rows)),
        grid_spec=pltpu.PrefetchScalarGridSpec(
            num_scalar_prefetch=3,
            grid=(n_src,),
            in_specs=[lists, lists]
            + [
                pl.BlockSpec((1, chunks, width, CHUNK), lambda s, *_, n=n: (jnp.clip(s - n * each, 0, each - 1), 0, 0, 0))
                for n in range(len(wide_rows))
            ]
            + [pl.BlockSpec(memory_space=pl.ANY)] * len(before),
            out_specs=pl.BlockSpec((entries // parts, width), lambda s, *_: (part, 0)),
        ),
        out_shape=jax.ShapeDtypeStruct((entries, width), jnp.float32),
        input_output_aliases={5 + len(wide_rows): 0} if before else {},
        compiler_params=pltpu.CompilerParams(vmem_limit_bytes=LIMIT),
        cost_estimate=pl.CostEstimate(flops=2 * 10**9 * n_src, bytes_accessed=5 * 10**6 * n_src, transcendentals=0),
        name="spread",
    )(pairs, counts, order, packed, weight, *wide_rows, *before)


def lists_kernel(ids_ref, place_ref, weight_ref, packed_ref, scaled_ref, ids, place, weight, out_packed, out_weight,
                 send_packed, recv_packed, send_weight, recv_weight, *, shards, owner_rows):
    row = lax.axis_index("rows")
    halves = packed_ref.shape[1]
    lines = ids_ref.shape[0]
    requests = lines * LANES
    barrier = pltpu.get_barrier_semaphore()

    def greet(s, _):
        pl.semaphore_signal(barrier, inc=1, device_id={"rows": lax.rem(row + s, shards)}, device_id_type=MESH)
        return 0

    lax.fori_loop(1, shards, greet, 0)
    ids[0:lines, :] = ids_ref[...]
    ids[lines:, :] = jnp.full((ids.shape[0] - lines, LANES), -1, jnp.int32)
    place[0:lines, :] = place_ref[...]
    place[lines:, :] = jnp.zeros((ids.shape[0] - lines, LANES), jnp.int32)
    weight[0:lines, :] = weight_ref[...]
    weight[lines:, :] = jnp.zeros((ids.shape[0] - lines, LANES), jnp.float32)

    def prepare(owner):
        below = jnp.sum(jnp.where(ids_ref[...] < owner * owner_rows, 1, 0))
        line = pl.ds((below // CHUNK) * HALVES, halves)
        own = ids[line, :] - owner * owner_rows
        inside = (own >= 0) & (own < owner_rows)
        out_packed[owner] = jnp.where(inside, own * requests + place[line, :], -requests)
        out_weight[owner] = weight[line, :]

    def copies(s):
        owner = lax.rem(row + s, shards)
        return [
            pltpu.make_async_remote_copy(
                src_ref=src.at[owner], dst_ref=dst.at[row], send_sem=send.at[s - 1], recv_sem=recv.at[s - 1],
                device_id={"rows": owner}, device_id_type=MESH,
            )
            for src, dst, send, recv in (
                (out_packed, packed_ref, send_packed, recv_packed),
                (out_weight, scaled_ref, send_weight, recv_weight),
            )
        ]

    prepare(lax.rem(row + 1, shards))
    pl.semaphore_wait(barrier, shards - 1)

    def send(s, _):
        for copy in copies(s):
            copy.start()
        prepare(lax.rem(row + s + 1, shards))
        return 0

    lax.fori_loop(1, shards, send, 0)
    packed_ref[row] = out_packed[row]
    scaled_ref[row] = out_weight[row]

    def finish(s, _):
        for copy in copies(s):
            copy.wait()
        return 0

    lax.fori_loop(1, shards, finish, 0)


def request_lists(memory_ids, score_cotangent, scale, owner_rows, shards):
    tokens, retrieved = memory_ids.shape
    requests = tokens * retrieved
    capacity = 3 * requests // (2 * shards)
    chunks = -(-(capacity + CHUNK - 1) // CHUNK)
    chains = min(CHAINS, chunks)
    chunks = -(-chunks // chains) * chains

    def line_up(values):
        tiles = values.reshape(retrieved // 8, 8, tokens // LANES, LANES)
        return tiles.transpose(0, 2, 1, 3).reshape(-1)

    flat = line_up(memory_ids.T)
    place = line_up(jnp.arange(requests, dtype=jnp.int32))
    weight = line_up(score_cotangent.T.astype(jnp.float32) * scale)
    ids, place, weight = lax.sort((flat, place, weight), num_keys=1, is_stable=False)
    lines = requests // LANES
    halves = chunks * HALVES
    whole = pl.BlockSpec(memory_space=pltpu.VMEM)
    dma = pltpu.SemaphoreType.DMA
    shape = (shards, halves, LANES)
    packed, weight = pl.pallas_call(
        functools.partial(lists_kernel, shards=shards, owner_rows=owner_rows),
        in_specs=[whole] * 3,
        out_specs=[whole] * 2,
        out_shape=[jax.ShapeDtypeStruct(shape, jnp.int32), jax.ShapeDtypeStruct(shape, jnp.float32)],
        scratch_shapes=[
            pltpu.VMEM((lines + halves, LANES), jnp.int32),
            pltpu.VMEM((lines + halves, LANES), jnp.int32),
            pltpu.VMEM((lines + halves, LANES), jnp.float32),
            pltpu.VMEM(shape, jnp.int32),
            pltpu.VMEM(shape, jnp.float32),
        ]
        + [dma((shards - 1,))] * 4,
        compiler_params=pltpu.CompilerParams(collective_id=1, has_side_effects=True, vmem_limit_bytes=32 * 2**20),
        cost_estimate=pl.CostEstimate(flops=10**7, bytes_accessed=3 * 10**6, transcendentals=0),
        name="lists",
    )(*(item.reshape(lines, LANES) for item in (ids, place, weight)))
    return packed, weight, chains


def pair_tables(packed, requests, owner_rows, parts):
    shards, halves, _ = packed.shape
    chunks = halves // HALVES
    windows = owner_rows // WINDOW
    entry = packed >> log2(requests)
    low = jnp.min(jnp.where(entry >= 0, entry, owner_rows), axis=2).reshape(shards, chunks, HALVES).min(axis=2) // WINDOW
    high = jnp.max(entry, axis=2).reshape(shards, chunks, HALVES).max(axis=2) // WINDOW + 1
    edge = jnp.arange(parts, dtype=jnp.int32)[:, None, None] * (windows // parts)
    low = jnp.maximum(low[None], edge)
    number = jnp.maximum(jnp.minimum(high[None], edge + windows // parts) - low, 0)
    upto = jnp.arange(chunks, dtype=jnp.int32)
    ends = jnp.sum(jnp.where(upto[:, None] <= upto[None, :], number[:, :, :, None], 0), axis=2)
    begins = ends - number
    most = -(-(chunks + windows // parts) // PAIRS) * PAIRS
    index = jnp.arange(most, dtype=jnp.int32)
    here = (index >= begins[..., None]) & (index < ends[..., None])
    value = upto[:, None] * 256 + (low - begins)[..., None] + index
    idle = (chunks - 1) * 256 + 255
    pairs = idle + jnp.sum(jnp.where(here, value - idle, 0), axis=2)
    used = jnp.max(jnp.where(number > 0, upto + 1, 0), axis=2)
    return pairs, ends[..., -1], used


def finish_kernel(
    part_ref, stats_ref, second_ref, small_ref, mid_ref, normed_ref, inv_ref, gain_ref, grad_ref, total_ref,
    got_part, got_stats, got_second, vector, got_vector,
    send_part, recv_part, send_stats, recv_stats, send_second, recv_second, send_vector, recv_vector,
    *, parts, shards, full_width
):
    me = lax.axis_index("tp")
    row = lax.axis_index("rows")
    width = mid_ref.shape[1]
    barrier = pltpu.get_barrier_semaphore()
    for s in range(1, parts):
        pl.semaphore_signal(barrier, inc=1, device_id={"tp": lax.rem(me + s, parts)}, device_id_type=MESH)

    def greet(s, _):
        pl.semaphore_signal(barrier, inc=1, device_id={"rows": lax.rem(row + s, shards)}, device_id_type=MESH)
        return 0

    lax.fori_loop(1, shards, greet, 0)
    pl.semaphore_wait(barrier, parts + shards - 2)

    copies = []
    for s in range(1, parts):
        peer = lax.rem(me + s, parts)
        columns = pl.ds(pl.multiple_of(peer * width, 128), width)
        for src, dst, send, recv in (
            (stats_ref, got_stats.at[s - 1], send_stats, recv_stats),
            (second_ref.at[:, columns], got_second.at[s - 1], send_second, recv_second),
            (part_ref.at[:, columns], got_part.at[s - 1], send_part, recv_part),
        ):
            copy = pltpu.make_async_remote_copy(
                src_ref=src, dst_ref=dst, send_sem=send.at[s - 1], recv_sem=recv.at[s - 1],
                device_id={"tp": peer}, device_id_type=MESH,
            )
            copy.start()
            copies.append(copy)
    own = pl.ds(pl.multiple_of(me * width, 128), width)
    for copy in copies:
        copy.wait()
    first = part_ref[:, own].astype(jnp.float32)
    stats = stats_ref[...]
    second = second_ref[:, own]
    for s in range(parts - 1):
        first = first + got_part[s].astype(jnp.float32)
        stats = stats + got_stats[s]
        second = second + got_second[s]
    stats = jnp.concatenate([stats] * (128 // stats.shape[0]), axis=0).T * (1.0 / full_width)
    normed = normed_ref[...]
    scaled = first * gain_ref[...]
    grad_ref[...] = mid_ref[...].astype(jnp.float32) + inv_ref[...] * (scaled - stats[:, 0:1] - normed * stats[:, 1:2])
    vector[0:8, :] = small_ref[...]
    vector[8:16, :] = second
    vector[16:24, :] = jnp.concatenate(
        [
            jnp.sum(first * normed, axis=0, keepdims=True),
            jnp.sum(first, axis=0, keepdims=True),
            jnp.zeros((6, width), jnp.float32),
        ],
        axis=0,
    )

    def to_row(s):
        return pltpu.make_async_remote_copy(
            src_ref=vector, dst_ref=got_vector.at[s - 1], send_sem=send_vector.at[s - 1], recv_sem=recv_vector.at[s - 1],
            device_id={"rows": lax.rem(row + s, shards)}, device_id_type=MESH,
        )

    def send(s, _):
        to_row(s).start()
        return 0

    lax.fori_loop(1, shards, send, 0)

    def await_row(s, _):
        to_row(s).wait()
        return 0

    lax.fori_loop(1, shards, await_row, 0)
    total_ref[...] = vector[...]

    def add(s, _):
        total_ref[...] += got_vector[s]
        return 0

    lax.fori_loop(0, shards - 1, add, 0)


def finish(part, stats, second, small, mid, normed, inv, gain, parts, shards):
    tokens, full_width = part.shape
    width = mid.shape[1]
    whole = pl.BlockSpec(memory_space=pltpu.VMEM)
    dma = pltpu.SemaphoreType.DMA
    return pl.pallas_call(
        functools.partial(finish_kernel, parts=parts, shards=shards, full_width=full_width),
        in_specs=[whole] * 8,
        out_specs=[whole] * 2,
        out_shape=[
            jax.ShapeDtypeStruct((tokens, width), jnp.float32),
            jax.ShapeDtypeStruct((24, width), jnp.float32),
        ],
        scratch_shapes=[
            pltpu.VMEM((parts - 1, tokens, width), part.dtype),
            pltpu.VMEM((parts - 1,) + stats.shape, jnp.float32),
            pltpu.VMEM((parts - 1, 8, width), jnp.float32),
            pltpu.VMEM((24, width), jnp.float32),
            pltpu.VMEM((shards - 1, 24, width), jnp.float32),
        ]
        + [dma((parts - 1,))] * 6
        + [dma((shards - 1,))] * 2,
        compiler_params=pltpu.CompilerParams(collective_id=0, has_side_effects=True, vmem_limit_bytes=32 * 2**20),
        cost_estimate=pl.CostEstimate(flops=10**7, bytes_accessed=8 * 10**6, transcendentals=0),
        name="finish",
    )(part, stats, second, small, mid, normed, inv, gain)


def normalize(values):
    row_mean = jnp.mean(values, axis=1, keepdims=True)
    centered = values - row_mean
    row_var = jnp.mean(centered * centered, axis=1, keepdims=True)
    inv_std = lax.rsqrt(row_var + 1e-05)
    return (centered * inv_std, inv_std)


def segment_of(lengths, row_count):
    places = jnp.arange(row_count, dtype=jnp.int32)
    bounds = jnp.cumsum(lengths)
    segment = jnp.sum((places[:, None] >= bounds[None, :]).astype(jnp.int32), axis=1)
    return (segment, places)


def permute(value, axis, step):
    size = lax.axis_size(axis)
    return lax.ppermute(value, axis, [(i, (i + step) % size) for i in range(size)])


def exchange(block_for, axis, stride=1):
    size = lax.axis_size(axis)
    me = lax.axis_index(axis)
    return [permute(block_for(lax.rem(me + s, size)), axis, s) for s in range(stride, size, stride)]


def gather(value, axis, dim):
    size = lax.axis_size(axis)
    me = lax.axis_index(axis)
    own = value.shape[dim]
    shape = value.shape[:dim] + (own * size,) + value.shape[dim + 1 :]
    whole = jnp.zeros(shape, value.dtype)
    for s, block in enumerate([value] + exchange(lambda q: value, axis)):
        whole = lax.dynamic_update_slice_in_dim(whole, block, lax.rem(me + size - s, size) * own, dim)
    return whole


def scatter_sum(value, axis, dim):
    size = lax.axis_size(axis)
    own = value.shape[dim] // size
    low = value.astype(jnp.bfloat16)
    total = lax.dynamic_slice_in_dim(value, lax.axis_index(axis) * own, own, dim).astype(jnp.float32)
    for block in exchange(lambda q: lax.dynamic_slice_in_dim(low, q * own, own, dim), axis):
        total = total + block.astype(jnp.float32)
    return total


def scatter_rows(value):
    return lax.psum_scatter(value.astype(jnp.bfloat16), "rows", scatter_dimension=0, tiled=True).astype(jnp.float32)


def pair_swap(value):
    size = lax.axis_size("rows")
    return lax.ppermute(value, "rows", [(i, i ^ 1) for i in range(size)])


def to_sources(parts, step):
    both = parts[0].astype(jnp.float32) + pair_swap(parts[1]).astype(jnp.float32)
    if step:
        both = permute(both.astype(parts.dtype), "rows", 2 * step).astype(jnp.float32)
    return both


def after(value, *others):
    return lax.optimization_barrier((value,) + others)[0]


def on_device(
    block_input,
    first_gain,
    first_shift,
    qkv_weight,
    qv_bias,
    out_weight,
    out_bias,
    second_gain,
    second_shift,
    up_weight,
    up_bias,
    down_weight,
    down_bias,
    memory_keys,
    memory_ids,
    doc_lengths,
    out_cotangent,
    score_cotangent,
):
    row_count, width = block_input.shape
    full_width = out_weight.shape[1]
    heads = width // HD
    shards = lax.axis_size("rows")
    parts = lax.axis_size("tp")
    retrieved = memory_ids.shape[1]
    owner_rows = memory_keys.shape[0]
    part = lax.axis_index("tp")
    offset = part * width
    own_tokens = row_count // parts
    token_offset = part * own_tokens
    head_scale = 1.0 / math.sqrt(HD)
    memory_scale = 1.0 / math.sqrt(full_width)

    def own_columns(values):
        return lax.dynamic_slice_in_dim(values, offset, width, values.ndim - 1)

    def own_rows(values):
        return lax.dynamic_slice_in_dim(values, token_offset, own_tokens, 0)

    def add_columns(whole, own):
        return lax.dynamic_update_slice_in_dim(whole, own_columns(whole) + own, offset, 1)

    inputs_full = gather(block_input, "tp", 1).astype(jnp.float32)
    packed, weight, chains = request_lists(memory_ids, score_cotangent, memory_scale, owner_rows, shards)
    requests = row_count * retrieved
    table = tuple(item[0] for item in pair_tables(packed, requests, owner_rows, 1))
    pieces = PARTS if owner_rows // WINDOW % PARTS == 0 else 1
    tables = pair_tables(packed, requests, owner_rows, pieces)[:2]
    direct = shards == 8
    here = lax.axis_index("rows")
    core = lax.rem(here, 2)
    if direct:
        steps = (1, 2, 3, 0)
        chips = [lax.rem(here // 2 + s, shards // 2) for s in steps]
        orders = [jnp.stack([2 * z + core, 2 * z + 1 - core]) for z in chips]
    else:
        steps = (0,)
        orders = [jnp.arange(shards, dtype=jnp.int32)]

    def fetch_from(n, start):
        return fetch(table, after(orders[n], start), packed, weight, memory_keys, row_count, retrieved, chains)

    normed_first, inv_first = normalize(inputs_full)
    normed_low = (normed_first * first_gain + first_shift).astype(jnp.bfloat16)
    qkv_flat = qkv_weight.transpose(1, 0, 2).reshape(full_width, 3 * width)
    projected = jnp.einsum("td,cde->cte", normed_low, qkv_weight, preferred_element_type=jnp.float32)
    query_heads = (projected[0] + qv_bias[0]).astype(jnp.bfloat16).reshape(row_count, heads, HD)
    key_heads = projected[1].astype(jnp.bfloat16).reshape(row_count, heads, HD)
    value_heads = (projected[2] + qv_bias[1]).astype(jnp.bfloat16).reshape(row_count, heads, HD)
    segment, places = segment_of(doc_lengths[0], row_count)
    allowed = (segment[:, None] == segment[None, :]) & (places[None, :] <= places[:, None])
    logits = jnp.einsum("qhd,khd->hqk", query_heads, key_heads, preferred_element_type=jnp.float32) * head_scale
    logits = jnp.where(allowed[None], logits, -1000000000.0)
    row_peak = jnp.max(logits, axis=2, keepdims=True)
    weights = jnp.exp(logits - row_peak)
    attention = weights / jnp.sum(weights, axis=2, keepdims=True)
    attention_low = attention.astype(jnp.bfloat16)
    mixed_heads = (
        jnp.einsum("hqk,khd->qhd", attention_low, value_heads, preferred_element_type=jnp.float32)
        .astype(jnp.bfloat16)
        .reshape(row_count, width)
    )
    attention_part = jnp.dot(mixed_heads, out_weight, preferred_element_type=jnp.float32)
    attention_part = add_columns(attention_part, jnp.broadcast_to(out_bias, (row_count, width)))
    attention_own = scatter_sum(attention_part, "tp", 0)

    found, grad_parts = [], []

    def fetch_next(n, start):
        if n < len(orders):
            found_part, grad_part = fetch_from(n, start)
            found.append(found_part)
            grad_parts.append(grad_part)
        return grad_parts[-1]

    done = fetch_next(0, attention_part)
    residual_mid = own_rows(inputs_full) + after(attention_own, done)
    normed_second, inv_second = normalize(residual_mid)
    second_own = (normed_second * second_gain + second_shift).astype(jnp.bfloat16)
    second_low = gather(second_own, "tp", 0)
    done = fetch_next(1, second_own)
    second_low = after(second_low, done)
    before = jnp.dot(second_low, up_weight, preferred_element_type=jnp.float32) + up_bias
    gelu_value, gelu_pull = jax.vjp(functools.partial(jax.nn.gelu, approximate=True), before)
    active = gelu_value.astype(jnp.bfloat16)
    down_part = jnp.dot(active, down_weight, preferred_element_type=jnp.float32)
    down_part = add_columns(down_part, jnp.broadcast_to(down_bias, (row_count, width)))
    down_part = lax.dynamic_update_slice_in_dim(down_part, own_rows(down_part) + residual_mid, token_offset, 0)
    output_own = scatter_sum(down_part, "tp", 1)
    done = fetch_next(2, down_part)
    output_low = after(output_own, done).astype(jnp.bfloat16)
    if direct:
        near = jnp.stack(exchange(lambda q: output_low, "rows", 2)[::-1] + [output_low])
    done = fetch_next(3, output_low)

    if direct:
        memory_part = sum(to_sources(grad_part, s) for grad_part, s in zip(grad_parts, steps))
        far = pair_swap(near)
        rows = [jnp.stack([near[2 * n : 2 * n + 2], far[2 * n : 2 * n + 2]], axis=1).reshape(4, row_count, width) for n in (0, 1)]
    else:
        memory_part = lax.psum_scatter(grad_parts[0].reshape(-1, width), "rows", scatter_dimension=0, tiled=True)
        rows = [lax.all_gather(output_low, "rows", axis=0, tiled=False)]
    grad_out = out_cotangent.astype(jnp.float32) + memory_part
    down_low = grad_out.astype(jnp.bfloat16)
    full_down = gather(down_low, "tp", 1)

    score_parts, wide_rows = [], []
    for n, rows_n in enumerate(rows):
        if direct:
            for m in (2 * n, 2 * n + 1):
                part_of = slice(2 * (m - 2 * n), 2 * (m - 2 * n) + 2)
                score_part, wide_part = score(table, orders[m], packed, found[m], rows_n[part_of], retrieved, chains)
                score_parts.append(score_part)
                wide_rows.append(wide_part)
        else:
            score_part, wide_part = score(table, orders[0], packed, found[0], rows_n, retrieved, chains)
            score_parts.append(score_part)
            wide_rows.append(wide_part)
    if direct:
        score_own = sum(to_sources(score_part, s) for score_part, s in zip(score_parts, steps))
    else:
        score_own = lax.psum_scatter(score_parts[0].reshape(-1, row_count), "rows", scatter_dimension=0, tiled=True)
    score_own = score_own + sum(exchange(lambda q: score_own, "tp"))
    memory_scores = score_own.T * memory_scale
    full_down = after(full_down, wide_rows[-1])

    order = jnp.concatenate(orders)
    shift = log2(requests)
    memory_grad = None

    def spread_next(first, last, memory_grad, *starts):
        for n in range(first, min(last, pieces)):
            memory_grad = spread(
                tables, after(order, *starts), packed, weight, wide_rows, owner_rows, shift, n, memory_grad
            )
        return memory_grad

    down_columns = own_columns(full_down).astype(jnp.float32)
    down_bias_grad = jnp.sum(down_columns, axis=0)
    down_weight_grad = jnp.einsum("td,tf->df", full_down, active, preferred_element_type=jnp.float32)
    down_weight_low = down_weight_grad.astype(jnp.bfloat16)
    down_weight_grad = scatter_rows(down_weight_low).T
    active_grad = jnp.einsum("td,fd->tf", full_down, down_weight, preferred_element_type=jnp.float32)
    before_grad = gelu_pull(active_grad)[0].astype(jnp.bfloat16)
    up_bias_grad = jnp.sum(before_grad.astype(jnp.float32), axis=0)
    up_weight_low = jnp.einsum("td,tf->df", second_low, before_grad, preferred_element_type=jnp.float32).astype(jnp.bfloat16)
    up_weight_grad = scatter_rows(up_weight_low)
    second_part = jnp.einsum("tf,df->td", before_grad, up_weight, preferred_element_type=jnp.float32)
    second_grad = scatter_sum(second_part, "tp", 0)
    memory_grad = spread_next(0, 1, memory_grad, second_part, up_weight_low, down_weight_low)
    second_grad = after(second_grad, memory_grad)
    scaled = second_grad * second_gain
    row_first = jnp.mean(scaled, axis=1, keepdims=True)
    row_second = jnp.mean(scaled * normed_second, axis=1, keepdims=True)
    mid_own = own_rows(full_down).astype(jnp.float32) + inv_second * (scaled - row_first - normed_second * row_second)
    second_norm_grads = jnp.stack([jnp.sum(second_grad * normed_second, axis=0), jnp.sum(second_grad, axis=0)])
    mid_low = mid_own.astype(jnp.bfloat16)
    full_mid = gather(mid_low, "tp", 0)
    memory_grad = spread_next(1, 2, memory_grad, mid_low)
    full_mid = after(full_mid, memory_grad)
    mid_columns = own_columns(full_mid)
    out_bias_grad = jnp.sum(mid_columns.astype(jnp.float32), axis=0)
    out_weight_grad = jnp.einsum("td,te->de", full_mid, mixed_heads, preferred_element_type=jnp.float32)
    out_weight_grad = scatter_rows(out_weight_grad).T
    mixed_grad = (
        jnp.einsum("td,ed->te", full_mid, out_weight, preferred_element_type=jnp.float32)
        .astype(jnp.bfloat16)
        .reshape(row_count, heads, HD)
    )
    grad_attention = jnp.einsum("qhd,khd->hqk", mixed_grad, value_heads, preferred_element_type=jnp.float32)
    row_delta = jnp.sum(attention * grad_attention, axis=2, keepdims=True)
    logit_grad = (attention * (grad_attention - row_delta)).astype(jnp.bfloat16)
    query_grad = jnp.einsum("hqk,khd->qhd", logit_grad, key_heads, preferred_element_type=jnp.float32) * head_scale
    key_grad = jnp.einsum("hqk,qhd->khd", logit_grad, query_heads, preferred_element_type=jnp.float32) * head_scale
    value_grad = jnp.einsum("hqk,qhd->khd", attention_low, mixed_grad, preferred_element_type=jnp.float32)
    stacked = jnp.concatenate(
        [item.astype(jnp.bfloat16).reshape(row_count, width) for item in (query_grad, key_grad, value_grad)], axis=1
    )
    qkv_low = jnp.einsum("td,te->de", normed_low, stacked, preferred_element_type=jnp.float32).astype(jnp.bfloat16)
    qkv_grad = scatter_rows(qkv_low).reshape(-1, 3, width).transpose(1, 0, 2)
    qv_part = jnp.stack([jnp.sum(stacked[:, c * width : (c + 1) * width].astype(jnp.float32), axis=0) for c in (0, 2)])
    first_part = jnp.einsum("te,de->td", stacked, qkv_flat, preferred_element_type=jnp.float32)
    first_scaled = first_part * first_gain
    row_parts = jnp.stack([jnp.sum(first_scaled, axis=1), jnp.sum(first_scaled * normed_first, axis=1)])
    eight = ((0, 6), (0, 0))
    small = jnp.concatenate(
        [qv_part, out_bias_grad[None], down_bias_grad[None], up_bias_grad.reshape(parts, width)], axis=0
    )
    first_low = first_part.astype(jnp.bfloat16)
    memory_grad = spread_next(2, PARTS, memory_grad, qkv_low)
    input_grad, totals = finish(
        after(first_low, memory_grad),
        jnp.pad(row_parts, eight),
        jnp.pad(second_norm_grads, eight),
        small,
        mid_columns,
        own_columns(normed_first),
        inv_first,
        own_columns(first_gain)[None],
        parts,
        shards,
    )
    return (
        output_low,
        memory_scores,
        input_grad,
        totals[16],
        totals[17],
        qkv_grad,
        totals[0:2],
        out_weight_grad,
        totals[2],
        totals[8],
        totals[9],
        up_weight_grad,
        totals[4:8].reshape(-1),
        down_weight_grad,
        totals[3],
        memory_grad,
    )


def solution(mesh):
    return jax.shard_map(
        on_device,
        mesh=mesh,
        in_specs=(
            P("rows", "tp"),
            P(),
            P(),
            P(None, None, "tp"),
            P(None, "tp"),
            P("tp", None),
            P("tp"),
            P(),
            P(),
            P(None, "tp"),
            P("tp"),
            P("tp", None),
            P("tp"),
            P("rows", "tp"),
            P("rows", None),
            P("rows", None),
            P("rows", "tp"),
            P("rows", None),
        ),
        out_specs=(
            P("rows", "tp"),
            P("rows", None),
            P("rows", "tp"),
            P("tp"),
            P("tp"),
            P(None, "rows", "tp"),
            P(None, "tp"),
            P("tp", "rows"),
            P("tp"),
            P("tp"),
            P("tp"),
            P("rows", "tp"),
            P("tp"),
            P("tp", "rows"),
            P("tp"),
            P("rows", "tp"),
        ),
        check_vma=False,
    )
```

```python
import functools
import math

import jax
import jax.numpy as jnp
from jax import lax
from jax.experimental import pallas as pl
from jax.experimental.pallas import tpu as pltpu
from jax.sharding import PartitionSpec as P

HD = 64
CHUNK = 256
WINDOW = 256
CHAINS = 5
CHIPS = 4
PAIRS = 26
LANES = 128
HALVES = CHUNK // LANES
PARTS = 1
SPREAD_PAIRS = 26
MESH = pl.DeviceIdType.MESH
NT = (((1,), (1,)), ((), ()))
TN = (((0,), (0,)), ((), ()))
LIMIT = 60 * 2**20


def log2(size):
    return size.bit_length() - 1


def slabs_of(entries):
    return next(n for n in (8, 5, 4, 2, 1) if entries // WINDOW % n == 0)


def one_hot(row, size, value=None):
    one = jnp.ones((1, row.shape[1]), jnp.bfloat16) if value is None else value.astype(jnp.bfloat16)
    place = lax.broadcasted_iota(jnp.int32, (256, row.shape[1]), 0).astype(jnp.bfloat16)
    parts = []
    for k in range(size // 256):
        near = jnp.clip(row - 256 * k, -1, 256).astype(jnp.bfloat16)
        parts.append(jnp.where(place == near, one, jnp.zeros((), jnp.bfloat16)))
    return parts[0] if len(parts) == 1 else jnp.concatenate(parts, axis=0)


def source(picks, here_ref, step):
    if picks is None:
        return step
    chip, core = here_ref[0] >> 1, here_ref[0] & 1
    places = [2 * lax.rem(chip + away, CHIPS) + (1 - core if far else core) for away, far in picks]
    return functools.reduce(lambda rest, k: jnp.where(step == k, places[k], rest), range(1, len(places)), places[0])


def pairs_at(pair_ref, src, step, number):
    pairs = [pair_ref[src, step * number + k] for k in range(number)]
    return [(pair >> 8, pair & 255) for pair in pairs]


def chunk_of(ref, c):
    return jnp.concatenate([ref[0, pl.ds(c * HALVES + k, 1), :] for k in range(HALVES)], axis=1)


def chunk_rows(ref, g, chains):
    return jnp.concatenate([chunk_of(ref, g * chains + k) for k in range(chains)], axis=1)


def fetch_kernel(
    pair_ref, count_ref, used_ref, here_ref, packed_ref, weight_ref, far_keys_ref, *refs, chains, retrieved, picks
):
    found_ref, grad_ref, token_ref, acc_ref, sum_ref, keys_ref, key_sems = refs[-7:]
    src = source(picks, here_ref, pl.program_id(0))
    tokens = grad_ref.shape[1]
    last = keys_ref.shape[0] // WINDOW - 1
    slabs = key_sems.shape[0]
    slab = keys_ref.shape[0] // slabs
    token_ref[...] = jnp.zeros(token_ref.shape, jnp.float32)

    def key_copy(k):
        rows = pl.ds(pl.multiple_of(k * slab, slab), slab)
        return pltpu.make_async_copy(far_keys_ref.at[rows, :], keys_ref.at[rows, :], key_sems.at[k])

    first = pl.program_id(0) == 0

    @pl.when(first)
    def _():
        for k in range(slabs):
            key_copy(k).start()

    def await_keys(have, need):
        def one(k, _):
            key_copy(k).wait()
            return 0

        lax.fori_loop(have, need, one, 0)
        return jnp.maximum(have, need)
    groups = (used_ref[src] + chains - 1) // chains
    sum_ref[...] = jnp.zeros(sum_ref.shape, jnp.float32)

    def clear(c, _):
        acc_ref[c] = jnp.zeros(acc_ref.shape[1:], jnp.float32)
        return 0

    lax.fori_loop(used_ref[src], groups * chains, clear, 0)

    def step(i, have):
        parts = []
        pairs = pairs_at(pair_ref, src, i, PAIRS)
        have = await_keys(have, functools.reduce(jnp.maximum, [jnp.minimum(b, last) for _, b in pairs]) * WINDOW // slab + 1)
        before = pair_ref[src, jnp.maximum(i * PAIRS - 1, 0)] >> 8
        before = jnp.where(i == 0, -1, before)
        for c, b in pairs:
            entry = chunk_of(packed_ref, c) >> log2(tokens * retrieved)
            keys = keys_ref[pl.ds(pl.multiple_of(jnp.minimum(b, last) * WINDOW, WINDOW), WINDOW), :]
            hot = one_hot(entry - b * WINDOW, WINDOW)
            parts.append((c, c == before, lax.dot_general(keys, hot, TN, preferred_element_type=jnp.float32)))
            before = c
        for c, more, part in parts:
            acc_ref[c] = jnp.where(more, acc_ref[c] + part, part)
        return have

    have = lax.fori_loop(0, (count_ref[src] + PAIRS - 1) // PAIRS, step, jnp.where(first, 0, slabs))
    await_keys(have, slabs)

    def group(g, _):
        found = jnp.concatenate([acc_ref[g * chains + k].astype(jnp.bfloat16) for k in range(chains)], axis=1)
        found_ref[0, g] = found
        token = chunk_rows(packed_ref, g, chains) & (tokens - 1)
        spread = one_hot(token, tokens, chunk_rows(weight_ref, g, chains))
        sum_ref[...] += lax.dot_general(spread, found, NT, preferred_element_type=jnp.float32)
        return 0

    lax.fori_loop(0, groups, group, 0)
    grad_ref[0] = sum_ref[...].astype(grad_ref.dtype)


def fetch(table, here, picks, packed, weight, keys, tokens, retrieved, chains, line, starts):
    n_src = packed.shape[0] if picks is None else len(picks)
    halves = packed.shape[1]
    chunks = halves // HALVES
    entries, width = keys.shape
    lists = pl.BlockSpec((1, halves, LANES), lambda s, pairs, counts, used, here: (source(picks, here, s), 0, 0))
    return pl.pallas_call(
        functools.partial(fetch_kernel, chains=chains, retrieved=retrieved, picks=picks),
        grid_spec=pltpu.PrefetchScalarGridSpec(
            num_scalar_prefetch=4,
            grid=(n_src,),
            in_specs=[lists, lists] + [pl.BlockSpec(memory_space=pl.ANY)] * (1 + len(starts)),
            out_specs=[
                pl.BlockSpec((1, chunks // chains, width, chains * CHUNK), lambda s, *_: (s, 0, 0, 0)),
                pl.BlockSpec((1, tokens, width), lambda s, *_: (s, 0, 0)),
                pl.BlockSpec((1, line), lambda s, *_: (0, 0)),
            ],
            scratch_shapes=[
                pltpu.VMEM((chunks, width, CHUNK), jnp.float32),
                pltpu.VMEM((tokens, width), jnp.float32),
                pltpu.VMEM((entries, width), keys.dtype),
                pltpu.SemaphoreType.DMA((slabs_of(entries),)),
            ],
        ),
        out_shape=[
            jax.ShapeDtypeStruct((n_src, chunks // chains, width, chains * CHUNK), jnp.bfloat16),
            jax.ShapeDtypeStruct((n_src, tokens, width), jnp.bfloat16),
            jax.ShapeDtypeStruct((1, line), jnp.float32),
        ],
        compiler_params=pltpu.CompilerParams(vmem_limit_bytes=LIMIT),
        cost_estimate=pl.CostEstimate(flops=12 * 10**9 * n_src, bytes_accessed=5 * 10**6 * n_src, transcendentals=0),
        name="fetch",
    )(*table, here, packed, weight, keys, *starts)


def score_kernel(used_ref, here_ref, packed_ref, found_ref, *refs, chains, retrieved, sources, picks):
    score_ref, wide_ref, token_ref, acc_ref, rows_ref = refs[-5:]
    for n, source_ref in enumerate(refs[:sources]):

        @pl.when((pl.program_id(0) == n) | (sources == 1))
        def _(source_ref=source_ref):
            rows_ref[...] = source_ref[0]

    token_ref[...] = jnp.zeros(token_ref.shape, jnp.float32)
    src = source(picks, here_ref, pl.program_id(0))
    tokens = rows_ref.shape[0]
    acc_ref[...] = jnp.zeros(acc_ref.shape, jnp.float32)

    def group(g, _):
        packed = chunk_rows(packed_ref, g, chains)
        token = packed & (tokens - 1)
        column = (packed >> log2(tokens)) & (retrieved - 1)
        pick = one_hot(token, tokens)
        wide = lax.dot_general(rows_ref[...], pick, TN, preferred_element_type=jnp.float32)
        for k in range(chains):
            wide_ref[0, g * chains + k] = wide[:, k * CHUNK : (k + 1) * CHUNK].astype(jnp.bfloat16)
        score = jnp.sum(found_ref[0, g].astype(jnp.float32) * wide, axis=0, keepdims=True)
        high = score.astype(jnp.bfloat16).astype(jnp.float32)
        at = lax.broadcasted_iota(jnp.int32, (retrieved, chains * CHUNK), 0) == column
        columns = jnp.concatenate([jnp.where(at, high, 0.0), jnp.where(at, score - high, 0.0)], axis=0)
        acc_ref[...] += lax.dot_general(columns.astype(jnp.bfloat16), pick, NT, preferred_element_type=jnp.float32)
        return 0

    lax.fori_loop(0, (used_ref[src] + chains - 1) // chains, group, 0)
    score_ref[0] = acc_ref[:retrieved, :] + acc_ref[retrieved:, :]


def score(table, here, picks, packed, found, pair, rows, retrieved, chains, line, starts):
    n_src = packed.shape[0] if picks is None else len(picks)
    halves = packed.shape[1]
    chunks = halves // HALVES
    _, tokens, width = rows[0][0].shape
    return pl.pallas_call(
        functools.partial(score_kernel, chains=chains, retrieved=retrieved, sources=len(rows), picks=picks),
        grid_spec=pltpu.PrefetchScalarGridSpec(
            num_scalar_prefetch=2,
            grid=(n_src,),
            in_specs=[
                pl.BlockSpec((1, halves, LANES), lambda s, used, here: (source(picks, here, s), 0, 0)),
                pl.BlockSpec((1, chunks // chains, width, chains * CHUNK), lambda s, *_: (pair * n_src + s, 0, 0, 0)),
            ]
            + [
                pl.BlockSpec((1, tokens, width), lambda s, *_, at=at: (s if at is None else at, 0, 0)) for _, at in rows
            ]
            + [pl.BlockSpec(memory_space=pl.ANY)] * len(starts),
            out_specs=[
                pl.BlockSpec((1, retrieved, tokens), lambda s, *_: (s, 0, 0)),
                pl.BlockSpec((1, chunks, width, CHUNK), lambda s, *_: (s, 0, 0, 0)),
                pl.BlockSpec((1, line), lambda s, *_: (0, 0)),
            ],
            scratch_shapes=[pltpu.VMEM((2 * retrieved, tokens), jnp.float32), pltpu.VMEM((tokens, width), jnp.bfloat16)],
        ),
        out_shape=[
            jax.ShapeDtypeStruct((n_src, retrieved, tokens), jnp.float32),
            jax.ShapeDtypeStruct((n_src, chunks, width, CHUNK), jnp.bfloat16),
            jax.ShapeDtypeStruct((1, line), jnp.float32),
        ],
        compiler_params=pltpu.CompilerParams(vmem_limit_bytes=LIMIT),
        cost_estimate=pl.CostEstimate(flops=8 * 10**9 * n_src, bytes_accessed=5 * 10**6 * n_src, transcendentals=0),
        name="score",
    )(table[2], here, packed, found, *(array for array, _ in rows), *starts)


def spread_kernel(pair_ref, count_ref, here_ref, packed_ref, weight_ref, *refs, shift, part, sources, picks):
    wide_refs, (far_mem_ref, token_ref, mem_ref, sems) = refs[:sources], refs[-4:]
    token_ref[...] = jnp.zeros(token_ref.shape, jnp.float32)
    final = pl.program_id(0) == pl.num_programs(0) - 1
    slabs = sems.shape[0]
    slab = mem_ref.shape[0] // slabs

    def store(k):
        rows = pl.ds(pl.multiple_of(k * slab, slab), slab)
        far_rows = pl.ds(pl.multiple_of(part * mem_ref.shape[0] + k * slab, slab), slab)
        return pltpu.make_async_copy(mem_ref.at[rows, :], far_mem_ref.at[far_rows, :], sems.at[k])

    def store_upto(had, upto):
        def one(k, _):
            store(k).start()
            return 0

        lax.fori_loop(had, upto, one, 0)
        return jnp.maximum(had, upto)
    each = pl.num_programs(0) // sources
    src = source(picks, here_ref, pl.program_id(0))
    windows = mem_ref.shape[0] // WINDOW

    def window(b):
        return pl.ds(pl.multiple_of(jnp.clip(b - part * windows, 0, windows - 1) * WINDOW, WINDOW), WINDOW)

    @pl.when(pl.program_id(0) == 0)
    def _():
        def clear(b, _):
            mem_ref[pl.ds(pl.multiple_of(b * WINDOW, WINDOW), WINDOW), :] = jnp.zeros((WINDOW, mem_ref.shape[1]), jnp.float32)
            return 0

        lax.fori_loop(0, windows, clear, 0)

    def step(wide_ref, i, had):
        parts = []
        for c, b in pairs_at(pair_ref, src, i, SPREAD_PAIRS):
            entry = chunk_of(packed_ref, c) >> shift
            hot = one_hot(entry - b * WINDOW, WINDOW, chunk_of(weight_ref, c))
            parts.append((b, lax.dot_general(hot, wide_ref[0, c], NT, preferred_element_type=jnp.float32)))
        for b, term in parts:
            mem_ref[window(b), :] += term
        most = pair_ref.shape[1] - 1
        ahead = jnp.clip((pair_ref[src, jnp.minimum((i + 1) * SPREAD_PAIRS, most)] & 255) - part * windows, 0, windows)
        return store_upto(had, jnp.where(final & (i + 1 < steps), ahead * WINDOW // slab, 0))

    steps = (count_ref[src] + SPREAD_PAIRS - 1) // SPREAD_PAIRS
    for n, wide_ref in enumerate(wide_refs):

        @pl.when(pl.program_id(0) // each == n)
        def _(wide_ref=wide_ref, n=n):
            had = lax.fori_loop(0, steps, functools.partial(step, wide_ref), 0)
            if n == len(wide_refs) - 1:

                @pl.when(final)
                def _():
                    store_upto(had, slabs)
                    for k in range(slabs):
                        store(k).wait()


def spread(tables, here, picks, packed, weight, wide_rows, entries, shift, part, partly, line, starts):
    n_src, halves, _ = packed.shape
    chunks = halves // HALVES
    width = wide_rows[0].shape[2]
    each = n_src // len(wide_rows)
    pairs, counts = (table[part] for table in tables)
    parts = tables[0].shape[0]
    lists = pl.BlockSpec((1, halves, LANES), lambda s, pairs, counts, here: (source(picks, here, s), 0, 0))
    before = [] if partly is None else [partly]
    return pl.pallas_call(
        functools.partial(spread_kernel, shift=shift, part=part, sources=len(wide_rows), picks=picks),
        grid_spec=pltpu.PrefetchScalarGridSpec(
            num_scalar_prefetch=3,
            grid=(n_src,),
            in_specs=[lists, lists]
            + [
                pl.BlockSpec((1, chunks, width, CHUNK), lambda s, *_, n=n: (jnp.clip(s - n * each, 0, each - 1), 0, 0, 0))
                for n in range(len(wide_rows))
            ]
            + [pl.BlockSpec(memory_space=pl.ANY)] * (len(before) + len(starts)),
            out_specs=[
                pl.BlockSpec(memory_space=pl.ANY),
                pl.BlockSpec((1, line), lambda s, *_: (0, 0)),
            ],
            scratch_shapes=[
                pltpu.VMEM((entries // parts, width), jnp.float32),
                pltpu.SemaphoreType.DMA((slabs_of(entries // parts),)),
            ],
        ),
        out_shape=[
            jax.ShapeDtypeStruct((entries, width), jnp.float32),
            jax.ShapeDtypeStruct((1, line), jnp.float32),
        ],
        input_output_aliases={5 + len(wide_rows): 0} if before else {},
        compiler_params=pltpu.CompilerParams(vmem_limit_bytes=LIMIT),
        cost_estimate=pl.CostEstimate(flops=9 * 10**9 * n_src, bytes_accessed=5 * 10**6 * n_src, transcendentals=0),
        name="spread",
    )(pairs, counts, here, packed, weight, *wide_rows, *before, *starts)


def lists_kernel(ids_ref, place_ref, weight_ref, mine_ref, gain_ref, shift_ref, *refs, shards, parts, owner_rows):
    block_refs, refs = refs[: parts - 1], refs[parts - 1 :]
    packed_ref, scaled_ref, residual_ref, normed_ref, inv_ref, low_ref, got = refs[:7]
    ids, place, weight, out_packed, out_weight = refs[7:12]
    send_packed, recv_packed, send_weight, recv_weight, send_block, recv_block = refs[12:]
    row = lax.axis_index("rows")
    me = lax.axis_index("tp")
    halves = packed_ref.shape[1]
    lines = ids_ref.shape[0]
    requests = lines * LANES
    barrier = pltpu.get_barrier_semaphore()

    def greet(s, _):
        pl.semaphore_signal(barrier, inc=1, device_id={"rows": lax.rem(row + s, shards)}, device_id_type=MESH)
        return 0

    lax.fori_loop(1, shards, greet, 0)
    for s in range(1, parts):
        pl.semaphore_signal(barrier, inc=1, device_id={"tp": lax.rem(me + s, parts)}, device_id_type=MESH)
    block_copies = [
        pltpu.make_async_remote_copy(
            src_ref=block_refs[s - 1], dst_ref=got.at[s - 1], send_sem=send_block.at[s - 1], recv_sem=recv_block.at[s - 1],
            device_id={"tp": lax.rem(me + s, parts)}, device_id_type=MESH,
        )
        for s in range(1, parts)
    ]
    ids[0:lines, :] = ids_ref[...]
    ids[lines:, :] = jnp.full((ids.shape[0] - lines, LANES), -1, jnp.int32)
    place[0:lines, :] = place_ref[...]
    place[lines:, :] = jnp.zeros((ids.shape[0] - lines, LANES), jnp.int32)
    weight[0:lines, :] = weight_ref[...]
    weight[lines:, :] = jnp.zeros((ids.shape[0] - lines, LANES), jnp.float32)

    def prepare(owner):
        below = jnp.sum(jnp.where(ids_ref[...] < owner * owner_rows, 1, 0))
        line = pl.ds((below // CHUNK) * HALVES, halves)
        own = ids[line, :] - owner * owner_rows
        inside = (own >= 0) & (own < owner_rows)
        out_packed[owner] = jnp.where(inside, own * requests + place[line, :], -requests)
        out_weight[owner] = weight[line, :]

    def copies(s):
        owner = lax.rem(row + s, shards)
        return [
            pltpu.make_async_remote_copy(
                src_ref=src.at[owner], dst_ref=dst.at[row], send_sem=send.at[s - 1], recv_sem=recv.at[s - 1],
                device_id={"rows": owner}, device_id_type=MESH,
            )
            for src, dst, send, recv in (
                (out_packed, packed_ref, send_packed, recv_packed),
                (out_weight, scaled_ref, send_weight, recv_weight),
            )
        ]

    prepare(lax.rem(row + 1, shards))
    pl.semaphore_wait(barrier, shards + parts - 2)
    for copy in block_copies:
        copy.start()

    def send(s, _):
        for copy in copies(s):
            copy.start()
        prepare(lax.rem(row + s + 1, shards))
        return 0

    lax.fori_loop(1, shards, send, 0)
    packed_ref[row] = out_packed[row]
    scaled_ref[row] = out_weight[row]

    def finish(s, _):
        for copy in copies(s):
            copy.wait()
        return 0

    for copy in block_copies:
        copy.wait()
    residual = functools.reduce(lambda a, b: a + b, [got[s].astype(jnp.float32) for s in range(parts - 1)], mine_ref[...])
    residual_ref[...] = residual
    residual = residual - jnp.mean(residual, axis=1, keepdims=True)
    inv = lax.rsqrt(jnp.mean(residual * residual, axis=1, keepdims=True) + 1e-05)
    normed = residual * inv
    inv_ref[...] = inv
    normed_ref[...] = normed
    low_ref[...] = (normed * gain_ref[...] + shift_ref[...]).astype(low_ref.dtype)
    lax.fori_loop(1, shards, finish, 0)


def request_lists(memory_ids, score_cotangent, scale, owner_rows, shards, mine, blocks, gain, shift):
    tokens, retrieved = memory_ids.shape
    requests = tokens * retrieved
    capacity = 3 * requests // (2 * shards)
    chunks = -(-(capacity + CHUNK - 1) // CHUNK)
    chains = min(CHAINS, chunks)
    chunks = -(-chunks // chains) * chains

    def line_up(values):
        tiles = values.reshape(retrieved // 8, 8, tokens // LANES, LANES)
        return tiles.transpose(0, 2, 1, 3).reshape(-1)

    flat = line_up(memory_ids.T)
    place = line_up(jnp.arange(requests, dtype=jnp.int32))
    weight = line_up(score_cotangent.T.astype(jnp.float32) * scale)
    ids, place, weight = lax.sort((flat, place, weight), num_keys=1, is_stable=False)
    lines = requests // LANES
    halves = chunks * HALVES
    whole = pl.BlockSpec(memory_space=pltpu.VMEM)
    dma = pltpu.SemaphoreType.DMA
    shape = (shards, halves, LANES)
    rows, full = mine.shape
    return chains, *pl.pallas_call(
        functools.partial(lists_kernel, shards=shards, parts=len(blocks) + 1, owner_rows=owner_rows),
        in_specs=[whole] * 6 + [pl.BlockSpec(memory_space=pltpu.HBM)] * len(blocks),
        out_specs=[whole] * 6,
        out_shape=[
            jax.ShapeDtypeStruct(shape, jnp.int32),
            jax.ShapeDtypeStruct(shape, jnp.float32),
            jax.ShapeDtypeStruct((rows, full), jnp.float32),
            jax.ShapeDtypeStruct((rows, full), jnp.float32),
            jax.ShapeDtypeStruct((rows, 1), jnp.float32),
            jax.ShapeDtypeStruct((rows, full), jnp.bfloat16),
        ],
        scratch_shapes=[
            pltpu.VMEM((len(blocks), rows, full), jnp.bfloat16),
            pltpu.VMEM((lines + halves, LANES), jnp.int32),
            pltpu.VMEM((lines + halves, LANES), jnp.int32),
            pltpu.VMEM((lines + halves, LANES), jnp.float32),
            pltpu.VMEM(shape, jnp.int32),
            pltpu.VMEM(shape, jnp.float32),
        ]
        + [dma((shards - 1,))] * 4
        + [dma((len(blocks),))] * 2,
        compiler_params=pltpu.CompilerParams(collective_id=1, has_side_effects=True, vmem_limit_bytes=LIMIT),
        cost_estimate=pl.CostEstimate(flops=14 * 10**9, bytes_accessed=3 * 10**6, transcendentals=0),
        name="lists",
    )(*(item.reshape(lines, LANES) for item in (ids, place, weight)), mine, gain, shift, *blocks)


def pair_tables(packed, requests, owner_rows, parts, step):
    shards, halves, _ = packed.shape
    chunks = halves // HALVES
    windows = owner_rows // WINDOW
    entry = packed >> log2(requests)
    low = jnp.min(jnp.where(entry >= 0, entry, owner_rows), axis=2).reshape(shards, chunks, HALVES).min(axis=2) // WINDOW
    high = jnp.max(entry, axis=2).reshape(shards, chunks, HALVES).max(axis=2) // WINDOW + 1
    edge = jnp.arange(parts, dtype=jnp.int32)[:, None, None] * (windows // parts)
    low = jnp.maximum(low[None], edge)
    number = jnp.maximum(jnp.minimum(high[None], edge + windows // parts) - low, 0)
    upto = jnp.arange(chunks, dtype=jnp.int32)
    ends = jnp.sum(jnp.where(upto[:, None] <= upto[None, :], number[:, :, :, None], 0), axis=2)
    begins = ends - number
    most = -(-(chunks + windows // parts) // step) * step
    index = jnp.arange(most, dtype=jnp.int32)
    here = (index >= begins[..., None]) & (index < ends[..., None])
    value = upto[:, None] * 256 + (low - begins)[..., None] + index
    idle = (chunks - 1) * 256 + 255
    pairs = idle + jnp.sum(jnp.where(here, value - idle, 0), axis=2)
    used = jnp.max(jnp.where(number > 0, upto + 1, 0), axis=2)
    return pairs, ends[..., -1], used


def finish_kernel(*refs, parts, shards, scores, full_width):
    score_refs, refs = refs[:scores], refs[scores:]
    other_refs, refs = refs[: parts - 1], refs[parts - 1 :]
    stats_ref, norm_ref, small_ref, mine_ref, middle_ref, normed_ref, inv_ref, gain_ref = refs[:8]
    total_ref, score_ref, input_ref, few, got_norm, got_few, vector, got_vector = refs[-14:-6]
    send_norm, recv_norm, send_few, recv_few, send_vector, recv_vector = refs[-6:]
    me = lax.axis_index("tp")
    row = lax.axis_index("rows")
    width = small_ref.shape[1]
    retrieved = score_ref.shape[0]
    barrier = pltpu.get_barrier_semaphore()
    for s in range(1, parts):
        pl.semaphore_signal(barrier, inc=1, device_id={"tp": lax.rem(me + s, parts)}, device_id_type=MESH)

    def greet(s, _):
        pl.semaphore_signal(barrier, inc=1, device_id={"rows": lax.rem(row + s, shards)}, device_id_type=MESH)
        return 0

    lax.fori_loop(1, shards, greet, 0)
    few[0:retrieved, :] = functools.reduce(lambda a, b: a + b, [ref[...] for ref in score_refs])
    few[retrieved:, :] = stats_ref[...]
    vector[0:8, :] = small_ref[...]
    pl.semaphore_wait(barrier, parts + shards - 2)

    def over_tp(s, src, dst, send, recv):
        return pltpu.make_async_remote_copy(
            src_ref=src, dst_ref=dst.at[s - 1], send_sem=send.at[s - 1], recv_sem=recv.at[s - 1],
            device_id={"tp": lax.rem(me + s, parts)}, device_id_type=MESH,
        )

    def columns(q):
        return pl.ds(pl.multiple_of(q * width, 128), width)

    copies = [
        over_tp(s, norm_ref.at[:, columns(lax.rem(me + s, parts))], got_norm, send_norm, recv_norm)
        for s in range(1, parts)
    ]
    few_copies = [over_tp(s, few, got_few, send_few, recv_few) for s in range(1, parts)]
    for copy in copies + few_copies:
        copy.start()
    for copy in copies:
        copy.wait()
    norms = norm_ref[:, columns(me)]
    for s in range(parts - 1):
        norms = norms + got_norm[s]
    vector[8:16, :] = norms

    def to_row(s):
        return pltpu.make_async_remote_copy(
            src_ref=vector, dst_ref=got_vector.at[s - 1], send_sem=send_vector.at[s - 1], recv_sem=recv_vector.at[s - 1],
            device_id={"rows": lax.rem(row + s, shards)}, device_id_type=MESH,
        )

    def send(s, _):
        to_row(s).start()
        return 0

    lax.fori_loop(1, shards, send, 0)
    for copy in few_copies:
        copy.wait()
    few_total = functools.reduce(lambda a, b: a + b, [got_few[s] for s in range(parts - 1)], few[...])
    score_ref[...] = few_total[0:retrieved, :] * (1.0 / math.sqrt(full_width))
    stats = few_total[retrieved:, :] * (1.0 / full_width)
    stats = jnp.concatenate([stats] * (LANES // stats.shape[0]), axis=0).T
    first = functools.reduce(lambda a, b: a + b, [ref[...].astype(jnp.float32) for ref in other_refs], mine_ref[...])
    scaled = first * gain_ref[...]
    input_ref[...] = middle_ref[...] + inv_ref[...] * (scaled - stats[:, 0:1] - normed_ref[...] * stats[:, 1:2])

    def await_row(s, _):
        to_row(s).wait()
        return 0

    lax.fori_loop(1, shards, await_row, 0)
    total_ref[...] = vector[...]

    def add(s, _):
        total_ref[...] += got_vector[s]
        return 0

    lax.fori_loop(0, shards - 1, add, 0)


def finish(scores, others, stats, norms, small, mine, middle, normed, inv, gain, starts, parts, shards):
    width = small.shape[1]
    few = (scores[0].shape[0] + stats.shape[0], stats.shape[1])
    whole = pl.BlockSpec(memory_space=pltpu.VMEM)
    dma = pltpu.SemaphoreType.DMA
    arrays = [*scores, *others, stats, norms, small, mine, middle, normed, inv, gain]
    return pl.pallas_call(
        functools.partial(finish_kernel, parts=parts, shards=shards, scores=len(scores), full_width=norms.shape[1]),
        in_specs=[whole] * len(arrays) + [pl.BlockSpec(memory_space=pl.ANY)] * len(starts),
        out_specs=[whole] * 3,
        out_shape=[
            jax.ShapeDtypeStruct((16, width), jnp.float32),
            jax.ShapeDtypeStruct(scores[0].shape, jnp.float32),
            jax.ShapeDtypeStruct(mine.shape, jnp.float32),
        ],
        scratch_shapes=[
            pltpu.VMEM(few, jnp.float32),
            pltpu.VMEM((parts - 1, 8, width), jnp.float32),
            pltpu.VMEM((parts - 1,) + few, jnp.float32),
            pltpu.VMEM((16, width), jnp.float32),
            pltpu.VMEM((shards - 1, 16, width), jnp.float32),
        ]
        + [dma((parts - 1,))] * 4
        + [dma((shards - 1,))] * 2,
        compiler_params=pltpu.CompilerParams(collective_id=0, has_side_effects=True, vmem_limit_bytes=LIMIT),
        cost_estimate=pl.CostEstimate(flops=16 * 10**9, bytes_accessed=10**6, transcendentals=0),
        name="finish",
    )(*arrays, *starts)


GELU_C = math.sqrt(2.0 / math.pi)
GELU_A = 0.044715


def place_rows(blocks, whole_ref):
    size, own = len(blocks), blocks[0].shape[0]
    me = lax.axis_index("tp")
    for s, block in enumerate(blocks):
        whole_ref[pl.ds(pl.multiple_of(lax.rem(me + size - s, size) * own, own), own), :] = block[...]


def place_columns(blocks, whole_ref):
    size, own = len(blocks), blocks[0].shape[1]
    me = lax.axis_index("tp")
    for s, block in enumerate(blocks):
        whole_ref[:, pl.ds(pl.multiple_of(lax.rem(me + size - s, size) * own, own), own)] = block[...]


def send_rows(whole_ref, own_ref, sends):
    size, own = len(sends) + 1, own_ref.shape[0]
    me = lax.axis_index("tp")

    def rows(s):
        return whole_ref[pl.ds(pl.multiple_of(lax.rem(me + s, size) * own, own), own), :]

    own_ref[...] = rows(0)
    for s, send in enumerate(sends):
        send[...] = rows(s + 1).astype(send.dtype)


def send_columns(whole_ref, own_ref, sends):
    size, own = len(sends) + 1, own_ref.shape[1]
    me = lax.axis_index("tp")

    def columns(s):
        return whole_ref[:, pl.ds(pl.multiple_of(lax.rem(me + s, size) * own, own), own)]

    own_ref[...] = columns(0)
    for s, send in enumerate(sends):
        send[...] = columns(s + 1).astype(send.dtype)


def visible(length_ref, first, rows, keys):
    row = lax.broadcasted_iota(jnp.int32, (rows, 1), 0) + first
    start, bound = jnp.zeros((rows, 1), jnp.int32), 0
    for k in range(length_ref.shape[1]):
        bound = bound + length_ref[0, k]
        start = jnp.where(row >= bound, bound, start)
    key = lax.broadcasted_iota(jnp.int32, (rows, keys), 1)
    return (key <= row) & (key >= start)


def head_lanes(h, width):
    lane = lax.broadcasted_iota(jnp.int32, (1, width), 1)
    return (lane >= h * HD) & (lane < (h + 1) * HD)


def attention_of(query, keys, seen):
    logits = lax.dot_general(query, keys, NT, preferred_element_type=jnp.float32) * (1.0 / math.sqrt(HD))
    logits = jnp.where(seen, logits, -1000000000.0)
    weights = jnp.exp(logits - jnp.max(logits, axis=1, keepdims=True))
    return weights / jnp.sum(weights, axis=1, keepdims=True)


def attend_kernel(length_ref, *refs, parts):
    blocks = refs[:parts]
    gain_ref, shift_ref, w_ref, qv_ref, out_ref, bias_ref = refs[parts : parts + 6]
    outs = refs[parts + 6 :]
    normed_ref, low_ref, inv_ref, qkv_ref, mixed_ref, own_ref = outs[:6]
    sends, (x_ref, part_ref) = outs[6:-2], outs[-2:]
    tokens, width = mixed_ref.shape
    place_columns(blocks, x_ref)
    x = x_ref[...].astype(jnp.float32)
    x = x - jnp.mean(x, axis=1, keepdims=True)
    inv = lax.rsqrt(jnp.mean(x * x, axis=1, keepdims=True) + 1e-05)
    normed = x * inv
    normed_ref[...] = normed
    inv_ref[...] = inv
    low = (normed * gain_ref[...] + shift_ref[...]).astype(jnp.bfloat16)
    low_ref[...] = low
    for c in range(3):
        value = jnp.dot(low, w_ref[c], preferred_element_type=jnp.float32)
        if c != 1:
            value = value + qv_ref[c // 2 : c // 2 + 1, :]
        qkv_ref[c] = value.astype(jnp.bfloat16)
    step = tokens // 2
    for first in (0, step):
        keys = first + step
        seen = visible(length_ref, first, step, keys)
        query = qkv_ref[0, first:keys, :]
        mixed = jnp.zeros((step, width), jnp.float32)
        for h in range(width // HD):
            lanes = head_lanes(h, width)
            attention = attention_of(jnp.where(lanes, query, jnp.zeros_like(query)), qkv_ref[1, :keys, :], seen)
            value = jnp.dot(attention.astype(jnp.bfloat16), qkv_ref[2, :keys, :], preferred_element_type=jnp.float32)
            mixed = jnp.where(lanes, value, mixed)
        mixed_ref[first:keys, :] = mixed.astype(jnp.bfloat16)
    part_ref[...] = jnp.dot(mixed_ref[...], out_ref[...], preferred_element_type=jnp.float32) + bias_ref[...]
    own = own_ref.shape[0]
    mine = pl.ds(pl.multiple_of(lax.axis_index("tp") * own, own), own)
    send_rows(part_ref, own_ref, sends)
    own_ref[...] += x_ref[mine, :].astype(jnp.float32)


def feed_kernel(*refs, parts):
    blocks = refs[:parts]
    residual_ref, up_ref, up_bias_ref, down_ref = refs[parts : parts + 4]
    outs = refs[parts + 4 :]
    low_ref, before_ref, active_ref, own_ref = outs[-5 - parts + 1 : -parts]
    sends, part_ref = outs[-parts:-1], outs[-1]
    place_rows(blocks, low_ref)
    before = jnp.dot(low_ref[...], up_ref[...], preferred_element_type=jnp.float32) + up_bias_ref[...]
    before_ref[...] = before
    bent = jnp.tanh(GELU_C * (before + GELU_A * before * before * before))
    active = (0.5 * before * (1.0 + bent)).astype(jnp.bfloat16)
    active_ref[...] = active
    part_ref[...] = jnp.dot(active, down_ref[...], preferred_element_type=jnp.float32)
    own = residual_ref.shape[0]
    mine = pl.ds(pl.multiple_of(lax.axis_index("tp") * own, own), own)
    part_ref[mine, :] += residual_ref[...]
    send_columns(part_ref, own_ref, sends)


def feed_back_kernel(*refs, parts):
    blocks = refs[:parts]
    low_ref, before_ref, active_ref, up_ref, down_ref = refs[parts : parts + 5]
    outs = refs[-7 - parts :]
    mine_ref, down_grad_ref, up_grad_ref, down_bias_ref, up_bias_ref, own_ref = outs[:6]
    sends, (full_ref, part_ref) = outs[6:-2], outs[-2:]
    place_columns(blocks, full_ref)
    own = mine_ref.shape[0]
    mine = pl.ds(pl.multiple_of(lax.axis_index("tp") * own, own), own)
    mine_ref[...] = full_ref[mine, :]
    down_bias_ref[...] = jnp.broadcast_to(
        jnp.sum(blocks[0][...].astype(jnp.float32), axis=0, keepdims=True), down_bias_ref.shape
    )
    active_grad = lax.dot_general(full_ref[...], down_ref[...], NT, preferred_element_type=jnp.float32)
    before = before_ref[...]
    bent = jnp.tanh(GELU_C * (before + GELU_A * before * before * before))
    slope = 0.5 * (1.0 + bent) + 0.5 * before * (1.0 - bent * bent) * GELU_C * (1.0 + 3.0 * GELU_A * before * before)
    grad = (active_grad * slope).astype(jnp.bfloat16)
    up_bias_ref[...] = jnp.broadcast_to(jnp.sum(grad.astype(jnp.float32), axis=0, keepdims=True), up_bias_ref.shape)
    part_ref[...] = lax.dot_general(grad, up_ref[...], NT, preferred_element_type=jnp.float32)
    send_rows(part_ref, own_ref, sends)
    down_grad_ref[...] = lax.dot_general(
        full_ref[...], active_ref[...], TN, preferred_element_type=jnp.float32
    ).astype(jnp.bfloat16)
    up_grad_ref[...] = lax.dot_general(low_ref[...], grad, TN, preferred_element_type=jnp.float32).astype(jnp.bfloat16)


def attend_back_kernel(length_ref, *refs, parts):
    blocks = refs[:parts]
    out_ref, qkv_ref, mixed_ref, w_ref, low_ref, normed_ref, gain_ref = refs[parts : parts + 7]
    second_gain_ref, second_shift_ref, down_bias_ref, up_bias_ref = refs[parts + 7 : parts + 11]
    outs = refs[-10 - parts :]
    middle_ref, normed_own_ref, gain_own_ref, weight_grad_ref, stats_ref, norm_ref, small_ref, own_ref = outs[:8]
    sends = outs[8 : 7 + parts]
    full_ref, part_ref, stacked_ref = outs[-3:]
    tokens, width = mixed_ref.shape
    place_rows(blocks, full_ref)
    columns = pl.ds(pl.multiple_of(lax.axis_index("tp") * width, width), width)
    middle_ref[...] = full_ref[:, columns].astype(jnp.float32)
    normed_own_ref[...] = normed_ref[:, columns]
    gain_own_ref[...] = gain_ref[:, columns]
    grad = lax.dot_general(full_ref[...], out_ref[...], NT, preferred_element_type=jnp.float32).astype(jnp.bfloat16)
    step = tokens // 2
    stacked_ref[...] = jnp.zeros(stacked_ref.shape, jnp.float32)
    scale = 1.0 / math.sqrt(HD)
    for first in (0, step):
        keys = first + step
        seen = visible(length_ref, first, step, keys)
        query = qkv_ref[0, first:keys, :]
        out_grad = grad[first:keys, :]
        key, value = qkv_ref[1, :keys, :], qkv_ref[2, :keys, :]
        for h in range(width // HD):
            lanes = head_lanes(h, width)
            query_h = jnp.where(lanes, query, jnp.zeros_like(query))
            grad_h = jnp.where(lanes, out_grad, jnp.zeros_like(out_grad))
            attention = attention_of(query_h, key, seen)
            attention_grad = lax.dot_general(grad_h, value, NT, preferred_element_type=jnp.float32)
            delta = jnp.sum(attention * attention_grad, axis=1, keepdims=True)
            logit_grad = (attention * (attention_grad - delta)).astype(jnp.bfloat16)
            query_grad = jnp.dot(logit_grad, key, preferred_element_type=jnp.float32) * scale
            stacked_ref[0, first:keys, :] += jnp.where(lanes, query_grad, 0.0)
            stacked_ref[1, :keys, :] += lax.dot_general(logit_grad, query_h, TN, preferred_element_type=jnp.float32) * scale
            stacked_ref[2, :keys, :] += lax.dot_general(
                attention.astype(jnp.bfloat16), grad_h, TN, preferred_element_type=jnp.float32
            )
    first_part = jnp.zeros(part_ref.shape, jnp.float32)
    small = []
    for c in range(3):
        item = stacked_ref[c].astype(jnp.bfloat16)
        small.append(jnp.sum(item.astype(jnp.float32), axis=0, keepdims=True))
        weight_grad_ref[:, c * width : (c + 1) * width] = lax.dot_general(
            low_ref[...], item, TN, preferred_element_type=jnp.float32
        ).astype(jnp.bfloat16)
        first_part += lax.dot_general(item, w_ref[c], NT, preferred_element_type=jnp.float32)
    part_ref[...] = first_part
    send_columns(part_ref, own_ref, sends)
    small_ref[...] = jnp.concatenate(
        [small[0], small[2], jnp.sum(middle_ref[...], axis=0, keepdims=True), down_bias_ref[0:1, :]]
        + [up_bias_ref[0:1, k * width : (k + 1) * width] for k in range(parts)],
        axis=0,
    )
    normed = normed_ref[...]
    norm_ref[...] = jnp.concatenate(
        [
            second_gain_ref[...],
            second_shift_ref[...],
            jnp.sum(first_part * normed, axis=0, keepdims=True),
            jnp.sum(first_part, axis=0, keepdims=True),
            jnp.zeros((4, first_part.shape[1]), jnp.float32),
        ],
        axis=0,
    )
    scaled = first_part * gain_ref[...]
    lane = lax.broadcasted_iota(jnp.int32, (1, LANES), 1)
    stats = jnp.where(lane == 0, jnp.sum(scaled, axis=1, keepdims=True), 0.0) + jnp.where(
        lane == 1, jnp.sum(scaled * normed, axis=1, keepdims=True), 0.0
    )
    stats_ref[...] = stats.T[0:8, :]
    weight_grad_ref[:, 3 * width :] = lax.dot_general(
        full_ref[...], mixed_ref[...], TN, preferred_element_type=jnp.float32
    ).astype(jnp.bfloat16)


def unpack_kernel(attend_ref, up_ref, down_ref, qkv_grad_ref, out_grad_ref, up_grad_ref, down_grad_ref, *, parts):
    width = out_grad_ref.shape[0]
    for c in range(3):
        qkv_grad_ref[c] = attend_ref[:, c * width : (c + 1) * width].astype(jnp.float32)
    out_grad_ref[...] = attend_ref[:, 3 * width :].astype(jnp.float32).T
    up_grad_ref[...] = up_ref[...].astype(jnp.float32)
    down_grad_ref[...] = down_ref[...].astype(jnp.float32).T


def block_call(name, kernel, lengths, arrays, starts, outs, scratch, flops, parts):
    whole = pl.BlockSpec(memory_space=pltpu.VMEM)
    scalars = [] if lengths is None else [lengths]
    return pl.pallas_call(
        functools.partial(kernel, parts=parts),
        in_specs=[pl.BlockSpec(memory_space=pltpu.SMEM)] * len(scalars)
        + [whole] * len(arrays)
        + [pl.BlockSpec(memory_space=pl.ANY)] * len(starts),
        out_specs=[whole] * len(outs),
        out_shape=[jax.ShapeDtypeStruct(shape, dtype) for shape, dtype in outs],
        scratch_shapes=[pltpu.VMEM(shape, dtype) for shape, dtype in scratch],
        compiler_params=pltpu.CompilerParams(vmem_limit_bytes=LIMIT),
        cost_estimate=pl.CostEstimate(flops=flops, bytes_accessed=10**7, transcendentals=0),
        name=name,
    )(*scalars, *arrays, *starts)


def permute(value, axis, step):
    size = lax.axis_size(axis)
    return lax.ppermute(value, axis, [(i, (i + step) % size) for i in range(size)])


def exchange(block_for, axis, stride=1):
    size = lax.axis_size(axis)
    me = lax.axis_index(axis)
    return [permute(block_for(lax.rem(me + s, size)), axis, s) for s in range(stride, size, stride)]


def deliver(sends):
    return [permute(block, "tp", s + 1) for s, block in enumerate(sends)]


def spread_out(value):
    return [value] + exchange(lambda q: value, "tp")


def total(mine, others, zero=None):
    first = mine.astype(jnp.float32)
    if zero is not None:
        first = first + zero[:, : mine.shape[-1]]
    return functools.reduce(lambda a, b: a + b.astype(jnp.float32), others, first)


def scatter_rows(value):
    return lax.psum_scatter(value, "rows", scatter_dimension=0, tiled=True)


def pair_swap(value):
    size = lax.axis_size("rows")
    return lax.ppermute(value, "rows", [(i, i ^ 1) for i in range(size)])


def on_device(
    block_input,
    first_gain,
    first_shift,
    qkv_weight,
    qv_bias,
    out_weight,
    out_bias,
    second_gain,
    second_shift,
    up_weight,
    up_bias,
    down_weight,
    down_bias,
    memory_keys,
    memory_ids,
    doc_lengths,
    out_cotangent,
    score_cotangent,
):
    row_count, width = block_input.shape
    full_width = out_weight.shape[1]
    shards = lax.axis_size("rows")
    parts = lax.axis_size("tp")
    retrieved = memory_ids.shape[1]
    owner_rows = memory_keys.shape[0]
    part = lax.axis_index("tp")
    offset = part * width
    own_tokens = row_count // parts
    memory_scale = 1.0 / math.sqrt(full_width)

    inputs = spread_out(block_input)

    f32, bf16 = jnp.float32, jnp.bfloat16
    bias_wide = lax.dynamic_update_slice_in_dim(jnp.zeros((1, full_width), f32), out_bias[None], offset, 1)
    normed_first, first_low, inv_first, qkv_low, mixed_heads, mine, *sends = block_call(
        "attend",
        attend_kernel,
        doc_lengths,
        [*inputs, first_gain[None], first_shift[None], qkv_weight, qv_bias, out_weight, bias_wide],
        [],
        [
            ((row_count, full_width), f32),
            ((row_count, full_width), bf16),
            ((row_count, 1), f32),
            ((3, row_count, width), bf16),
            ((row_count, width), bf16),
            ((own_tokens, full_width), f32),
        ]
        + [((own_tokens, full_width), bf16)] * (parts - 1),
        [((row_count, full_width), bf16), ((row_count, full_width), f32)],
        9 * 10**9,
        parts,
    )

    chains, packed, weight, residual_mid, normed_second, inv_second, second_own = request_lists(
        memory_ids,
        score_cotangent,
        memory_scale,
        owner_rows,
        shards,
        mine,
        sends,
        second_gain[None],
        second_shift[None],
    )
    requests = row_count * retrieved
    shift = log2(requests)
    table = tuple(item[0] for item in pair_tables(packed, requests, owner_rows, 1, PAIRS))
    pieces = PARTS if owner_rows // WINDOW % PARTS == 0 else 1
    tables = pair_tables(packed, requests, owner_rows, pieces, SPREAD_PAIRS)[:2]
    direct = shards == 2 * CHIPS
    here = lax.axis_index("rows").astype(jnp.int32)[None]
    near, far = ([(away, other) for away in (1, 2, 3, 0)] for other in (False, True))
    if direct:
        orders = [far[:2] + near[:2], far[2:], near[2:]]
        score_orders = [near[:2], near[2:], far[:2], far[2:]]
    else:
        orders = score_orders = [None]
    found, grads, zeros = [], [], []

    def fetch_next(*starts):
        n = len(found)
        if n < len(orders):
            found_part, grad_part, token = fetch(
                table, here, orders[n], packed, weight, memory_keys, row_count, retrieved, chains, full_width, starts
            )
            found.append(found_part)
            grads.append(grad_part)
            zeros.append(token)
        return zeros[-1]

    seconds = spread_out(second_own)
    fetch_next(second_own)
    second_low, before, active, mine, *sends = block_call(
        "feed",
        feed_kernel,
        None,
        [*seconds, residual_mid, up_weight, up_bias[None], down_weight],
        [grads[-1]],
        [
            ((row_count, full_width), bf16),
            ((row_count, up_bias.shape[0]), f32),
            ((row_count, up_bias.shape[0]), bf16),
            ((row_count, width), f32),
        ]
        + [((row_count, width), bf16)] * (parts - 1),
        [((row_count, full_width), f32)],
        8 * 10**9,
        parts,
    )
    others = deliver(sends)
    if direct:
        twin = pair_swap(grads[0][:2])
        summed = [total(grads[0][2 + n], [twin[n]]).astype(bf16) for n in (0, 1)]
        moved = [permute(summed[n], "rows", 2 * (n + 1)) for n in (0, 1)]
    zero = fetch_next(mine, *(summed if direct else ()))
    output_low = (total(mine, others, zero) + down_bias).astype(jnp.bfloat16)
    if direct:
        twin = pair_swap(grads[1])
        rows_near = exchange(lambda q: output_low, "rows", 2)[::-1]
        zero = fetch_next(output_low)
        rows_near = [row[None] for row in rows_near] + [output_low[None]]
        rows_far = pair_swap(jnp.concatenate(rows_near))
        score_rows = [
            [(rows_near[0], 0), (rows_near[1], 0)],
            [(rows_near[2], 0), (rows_near[3], 0)],
            [(rows_far, 0), (rows_far, 1)],
            [(rows_far, 2), (rows_far, 3)],
        ]
        moved.append(permute(total(grads[2][0], [twin[0]], zero).astype(bf16), "rows", 6))
        mine = total(grads[2][1], [twin[1]])
        score_found = [(found[0], 1), (found[2], 0), (found[0], 0), (found[1], 0)]
    else:
        memory_part = lax.psum_scatter(grads[0].reshape(-1, width), "rows", scatter_dimension=0, tiled=True)
        score_rows = [[(lax.all_gather(output_low, "rows", axis=0, tiled=False), None)]]
        score_found = [(found[0], 0)]
    score_parts, wide_rows = [], []

    def score_next(*starts):
        n = len(score_parts)
        if n < len(score_orders):
            score_part, wide_part, token = score(
                table, here, score_orders[n], packed, *score_found[n], score_rows[n], retrieved, chains, full_width, starts
            )
            score_parts.append(score_part)
            wide_rows.append(wide_part)
            zeros.append(token)
        return zeros[-1]

    zero = score_next(grads[-1])
    if direct:
        memory_part = total(mine, moved, zero)
    grad_out = out_cotangent.astype(jnp.float32) + memory_part
    down_low = grad_out.astype(jnp.bfloat16)
    downs = spread_out(down_low)
    score_next(down_low)
    down_mine, down_weight_low, up_weight_low, down_bias_grad, up_bias_grad, mine, *sends = block_call(
        "feed_back",
        feed_back_kernel,
        None,
        [*downs, second_low, before, active, up_weight, down_weight],
        [wide_rows[-1]],
        [
            ((own_tokens, full_width), bf16),
            ((full_width, up_bias.shape[0]), bf16),
            ((full_width, up_bias.shape[0]), bf16),
            ((8, width), f32),
            ((8, up_bias.shape[0]), f32),
            ((own_tokens, full_width), f32),
        ]
        + [((own_tokens, full_width), bf16)] * (parts - 1),
        [((row_count, full_width), bf16), ((row_count, full_width), f32)],
        14 * 10**9,
        parts,
    )
    others = deliver(sends)
    down_weight_grad = scatter_rows(down_weight_low)
    up_weight_grad = scatter_rows(up_weight_low)
    if direct:
        score_next(mine, down_weight_low, up_weight_low)
    second_grad = total(mine, others, zeros[-1])
    scaled = second_grad * second_gain
    row_first = jnp.mean(scaled, axis=1, keepdims=True)
    row_second = jnp.mean(scaled * normed_second, axis=1, keepdims=True)
    mid_own = down_mine.astype(jnp.float32) + inv_second * (scaled - row_first - normed_second * row_second)
    second_norm_grads = [jnp.sum(item, axis=0, keepdims=True) for item in (second_grad * normed_second, second_grad)]
    mid_low = mid_own.astype(jnp.bfloat16)
    order = sum(score_orders, []) if direct else None
    partly = []

    def spread_next(*starts):
        n = len(partly)
        if n < pieces:
            mem, token = spread(
                tables, here, order, packed, weight, wide_rows, owner_rows, shift, n, partly[-1] if n else None, full_width, starts
            )
            partly.append(mem)
            zeros.append(token)
        return zeros[-1]

    middles = spread_out(mid_low)
    if direct:
        score_next(mid_low)
        score_twin = [pair_swap(score_part) for score_part in score_parts[2:]]
        score_sum = [total(score_parts[0], score_twin[:1], zeros[-1][:, :row_count])]
    mid_columns, normed_own, gain_own, attend_low, row_parts, norm_parts, small, mine, *sends = block_call(
        "attend_back",
        attend_back_kernel,
        doc_lengths,
        [*middles, out_weight, qkv_low, mixed_heads, qkv_weight, first_low, normed_first, first_gain[None]]
        + [*second_norm_grads, down_bias_grad, up_bias_grad],
        [score_sum[0], down_weight_grad] if direct else [],
        [
            ((row_count, width), f32),
            ((row_count, width), f32),
            ((1, width), f32),
            ((full_width, 4 * width), bf16),
            ((8, row_count), f32),
            ((8, full_width), f32),
            ((8, width), f32),
            ((row_count, width), f32),
        ]
        + [((row_count, width), bf16)] * (parts - 1),
        [((row_count, full_width), bf16), ((row_count, full_width), f32), ((3, row_count, width), f32)],
        14 * 10**9,
        parts,
    )
    others = deliver(sends)
    if direct:
        score_sum.append(total(score_parts[1], score_twin[1:], row_parts[2:3]))
        score_moved = [permute(score_sum[n // 2][n % 2], "rows", 2 * (n + 1)) for n in range(3)]
    attend_grad = scatter_rows(attend_low)
    if direct:
        scores = [score_sum[1][1], *score_moved]
    else:
        scores = [lax.psum_scatter(score_parts[0].reshape(-1, row_count), "rows", scatter_dimension=0, tiled=True)]
    zero = spread_next(mine, *([*score_moved[:2], score_sum[1]] if direct else []))
    totals, memory_scores, input_grad = finish(
        scores,
        others,
        row_parts,
        norm_parts,
        small,
        mine,
        mid_columns,
        normed_own,
        inv_first,
        gain_own,
        [zero],
        parts,
        shards,
    )
    own_rows, up_width = up_weight_grad.shape
    qkv_grad, out_weight_grad, up_weight_grad, down_weight_grad = block_call(
        "unpack",
        unpack_kernel,
        None,
        [attend_grad, up_weight_grad, down_weight_grad],
        [],
        [((3, own_rows, width), f32), ((width, own_rows), f32), ((own_rows, up_width), f32), ((up_width, own_rows), f32)],
        [],
        3 * 10**9,
        parts,
    )
    return (
        output_low,
        memory_scores.T,
        input_grad,
        totals[10],
        totals[11],
        qkv_grad,
        totals[0:2],
        out_weight_grad,
        totals[2],
        totals[8],
        totals[9],
        up_weight_grad,
        totals[4:8].reshape(-1),
        down_weight_grad,
        totals[3],
        partly[-1],
    )


def solution(mesh):
    return jax.shard_map(
        on_device,
        mesh=mesh,
        in_specs=(
            P("rows", "tp"),
            P(),
            P(),
            P(None, None, "tp"),
            P(None, "tp"),
            P("tp", None),
            P("tp"),
            P(),
            P(),
            P(None, "tp"),
            P("tp"),
            P("tp", None),
            P("tp"),
            P("rows", "tp"),
            P("rows", None),
            P("rows", None),
            P("rows", "tp"),
            P("rows", None),
        ),
        out_specs=(
            P("rows", "tp"),
            P("rows", None),
            P("rows", "tp"),
            P("tp"),
            P("tp"),
            P(None, "rows", "tp"),
            P(None, "tp"),
            P("tp", "rows"),
            P("tp"),
            P("tp"),
            P("tp"),
            P("rows", "tp"),
            P("tp"),
            P("tp", "rows"),
            P("tp"),
            P("rows", "tp"),
        ),
        check_vma=False,
    )
```

```python
import functools
import math

import jax
import jax.numpy as jnp
from jax import lax
from jax.experimental import pallas as pl
from jax.experimental.pallas import tpu as pltpu
from jax.sharding import PartitionSpec as P

HD = 64
CHUNK = 256
WINDOW = 256
CHAINS = 5
CHIPS = 4
PAIRS = 26
LANES = 128
HALVES = CHUNK // LANES
PARTS = 1
SPREAD_PAIRS = 26
MESH = pl.DeviceIdType.MESH
NT = (((1,), (1,)), ((), ()))
TN = (((0,), (0,)), ((), ()))
LIMIT = 60 * 2**20


def log2(size):
    return size.bit_length() - 1


def slabs_of(entries):
    return next(n for n in (8, 5, 4, 2, 1) if entries // WINDOW % n == 0)


def one_hot(row, size, value=None):
    one = jnp.ones((1, row.shape[1]), jnp.bfloat16) if value is None else value.astype(jnp.bfloat16)
    place = lax.broadcasted_iota(jnp.int32, (256, row.shape[1]), 0).astype(jnp.bfloat16)
    parts = []
    for k in range(size // 256):
        near = jnp.clip(row - 256 * k, -1, 256).astype(jnp.bfloat16)
        parts.append(jnp.where(place == near, one, jnp.zeros((), jnp.bfloat16)))
    return parts[0] if len(parts) == 1 else jnp.concatenate(parts, axis=0)


def source(picks, here_ref, step):
    if picks is None:
        return step
    chip, core = here_ref[0] >> 1, here_ref[0] & 1
    places = [2 * lax.rem(chip + away, CHIPS) + (1 - core if far else core) for away, far in picks]
    return functools.reduce(lambda rest, k: jnp.where(step == k, places[k], rest), range(1, len(places)), places[0])


def pairs_at(pair_ref, src, step, number):
    pairs = [pair_ref[src, step * number + k] for k in range(number)]
    return [(pair >> 8, pair & 255) for pair in pairs]


def chunk_of(ref, c):
    return jnp.concatenate([ref[0, pl.ds(c * HALVES + k, 1), :] for k in range(HALVES)], axis=1)


def chunk_rows(ref, g, chains):
    return jnp.concatenate([chunk_of(ref, g * chains + k) for k in range(chains)], axis=1)


def fetch_kernel(
    pair_ref, count_ref, used_ref, here_ref, packed_ref, weight_ref, far_keys_ref, *refs, chains, retrieved, picks
):
    found_ref, grad_ref, token_ref, acc_ref, sum_ref, keys_ref, key_sems = refs[-7:]
    src = source(picks, here_ref, pl.program_id(0))
    tokens = grad_ref.shape[1]
    last = keys_ref.shape[0] // WINDOW - 1
    slabs = key_sems.shape[0]
    slab = keys_ref.shape[0] // slabs
    token_ref[...] = jnp.zeros(token_ref.shape, jnp.float32)

    def key_copy(k):
        rows = pl.ds(pl.multiple_of(k * slab, slab), slab)
        return pltpu.make_async_copy(far_keys_ref.at[rows, :], keys_ref.at[rows, :], key_sems.at[k])

    first = pl.program_id(0) == 0

    @pl.when(first)
    def _():
        for k in range(slabs):
            key_copy(k).start()

    def await_keys(have, need):
        def one(k, _):
            key_copy(k).wait()
            return 0

        lax.fori_loop(have, need, one, 0)
        return jnp.maximum(have, need)
    groups = (used_ref[src] + chains - 1) // chains
    sum_ref[...] = jnp.zeros(sum_ref.shape, jnp.float32)

    def clear(c, _):
        acc_ref[c] = jnp.zeros(acc_ref.shape[1:], jnp.float32)
        return 0

    lax.fori_loop(used_ref[src], groups * chains, clear, 0)

    def step(i, have):
        parts = []
        pairs = pairs_at(pair_ref, src, i, PAIRS)
        have = await_keys(have, functools.reduce(jnp.maximum, [jnp.minimum(b, last) for _, b in pairs]) * WINDOW // slab + 1)
        before = pair_ref[src, jnp.maximum(i * PAIRS - 1, 0)] >> 8
        before = jnp.where(i == 0, -1, before)
        for c, b in pairs:
            entry = chunk_of(packed_ref, c) >> log2(tokens * retrieved)
            keys = keys_ref[pl.ds(pl.multiple_of(jnp.minimum(b, last) * WINDOW, WINDOW), WINDOW), :]
            hot = one_hot(entry - b * WINDOW, WINDOW)
            parts.append((c, c == before, lax.dot_general(keys, hot, TN, preferred_element_type=jnp.float32)))
            before = c
        for c, more, part in parts:
            acc_ref[c] = jnp.where(more, acc_ref[c] + part, part)
        return have

    have = lax.fori_loop(0, (count_ref[src] + PAIRS - 1) // PAIRS, step, jnp.where(first, 0, slabs))
    await_keys(have, slabs)

    def group(g, _):
        found = jnp.concatenate([acc_ref[g * chains + k].astype(jnp.bfloat16) for k in range(chains)], axis=1)
        found_ref[0, g] = found
        token = chunk_rows(packed_ref, g, chains) & (tokens - 1)
        spread = one_hot(token, tokens, chunk_rows(weight_ref, g, chains))
        sum_ref[...] += lax.dot_general(spread, found, NT, preferred_element_type=jnp.float32)
        return 0

    lax.fori_loop(0, groups, group, 0)
    grad_ref[0] = sum_ref[...].astype(grad_ref.dtype)


def fetch(table, here, picks, packed, weight, keys, tokens, retrieved, chains, line, starts):
    n_src = packed.shape[0] if picks is None else len(picks)
    halves = packed.shape[1]
    chunks = halves // HALVES
    entries, width = keys.shape
    lists = pl.BlockSpec((1, halves, LANES), lambda s, pairs, counts, used, here: (source(picks, here, s), 0, 0))
    return pl.pallas_call(
        functools.partial(fetch_kernel, chains=chains, retrieved=retrieved, picks=picks),
        grid_spec=pltpu.PrefetchScalarGridSpec(
            num_scalar_prefetch=4,
            grid=(n_src,),
            in_specs=[lists, lists] + [pl.BlockSpec(memory_space=pl.ANY)] * (1 + len(starts)),
            out_specs=[
                pl.BlockSpec((1, chunks // chains, width, chains * CHUNK), lambda s, *_: (s, 0, 0, 0)),
                pl.BlockSpec((1, tokens, width), lambda s, *_: (s, 0, 0)),
                pl.BlockSpec((1, line), lambda s, *_: (0, 0)),
            ],
            scratch_shapes=[
                pltpu.VMEM((chunks, width, CHUNK), jnp.float32),
                pltpu.VMEM((tokens, width), jnp.float32),
                pltpu.VMEM((entries, width), keys.dtype),
                pltpu.SemaphoreType.DMA((slabs_of(entries),)),
            ],
        ),
        out_shape=[
            jax.ShapeDtypeStruct((n_src, chunks // chains, width, chains * CHUNK), jnp.bfloat16),
            jax.ShapeDtypeStruct((n_src, tokens, width), jnp.bfloat16),
            jax.ShapeDtypeStruct((1, line), jnp.float32),
        ],
        compiler_params=pltpu.CompilerParams(vmem_limit_bytes=LIMIT),
        cost_estimate=pl.CostEstimate(flops=12 * 10**9 * n_src, bytes_accessed=5 * 10**6 * n_src, transcendentals=0),
        name="fetch",
    )(*table, here, packed, weight, keys, *starts)


def score_kernel(used_ref, here_ref, packed_ref, found_ref, *refs, chains, retrieved, sources, picks):
    score_ref, wide_ref, token_ref, acc_ref, rows_ref = refs[-5:]
    for n, source_ref in enumerate(refs[:sources]):

        @pl.when((pl.program_id(0) == n) | (sources == 1))
        def _(source_ref=source_ref):
            rows_ref[...] = source_ref[0]

    token_ref[...] = jnp.zeros(token_ref.shape, jnp.float32)
    src = source(picks, here_ref, pl.program_id(0))
    tokens = rows_ref.shape[0]
    acc_ref[...] = jnp.zeros(acc_ref.shape, jnp.float32)

    def group(g, _):
        packed = chunk_rows(packed_ref, g, chains)
        token = packed & (tokens - 1)
        column = (packed >> log2(tokens)) & (retrieved - 1)
        pick = one_hot(token, tokens)
        wide = lax.dot_general(rows_ref[...], pick, TN, preferred_element_type=jnp.float32)
        for k in range(chains):
            wide_ref[0, g * chains + k] = wide[:, k * CHUNK : (k + 1) * CHUNK].astype(jnp.bfloat16)
        score = jnp.sum(found_ref[0, g].astype(jnp.float32) * wide, axis=0, keepdims=True)
        high = score.astype(jnp.bfloat16).astype(jnp.float32)
        at = lax.broadcasted_iota(jnp.int32, (retrieved, chains * CHUNK), 0) == column
        columns = jnp.concatenate([jnp.where(at, high, 0.0), jnp.where(at, score - high, 0.0)], axis=0)
        acc_ref[...] += lax.dot_general(columns.astype(jnp.bfloat16), pick, NT, preferred_element_type=jnp.float32)
        return 0

    lax.fori_loop(0, (used_ref[src] + chains - 1) // chains, group, 0)
    score_ref[0] = acc_ref[:retrieved, :] + acc_ref[retrieved:, :]


def score(table, here, picks, packed, found, pair, rows, retrieved, chains, line, starts):
    n_src = packed.shape[0] if picks is None else len(picks)
    halves = packed.shape[1]
    chunks = halves // HALVES
    _, tokens, width = rows[0][0].shape
    return pl.pallas_call(
        functools.partial(score_kernel, chains=chains, retrieved=retrieved, sources=len(rows), picks=picks),
        grid_spec=pltpu.PrefetchScalarGridSpec(
            num_scalar_prefetch=2,
            grid=(n_src,),
            in_specs=[
                pl.BlockSpec((1, halves, LANES), lambda s, used, here: (source(picks, here, s), 0, 0)),
                pl.BlockSpec((1, chunks // chains, width, chains * CHUNK), lambda s, *_: (pair * n_src + s, 0, 0, 0)),
            ]
            + [
                pl.BlockSpec((1, tokens, width), lambda s, *_, at=at: (s if at is None else at, 0, 0)) for _, at in rows
            ]
            + [pl.BlockSpec(memory_space=pl.ANY)] * len(starts),
            out_specs=[
                pl.BlockSpec((1, retrieved, tokens), lambda s, *_: (s, 0, 0)),
                pl.BlockSpec((1, chunks, width, CHUNK), lambda s, *_: (s, 0, 0, 0)),
                pl.BlockSpec((1, line), lambda s, *_: (0, 0)),
            ],
            scratch_shapes=[pltpu.VMEM((2 * retrieved, tokens), jnp.float32), pltpu.VMEM((tokens, width), jnp.bfloat16)],
        ),
        out_shape=[
            jax.ShapeDtypeStruct((n_src, retrieved, tokens), jnp.float32),
            jax.ShapeDtypeStruct((n_src, chunks, width, CHUNK), jnp.bfloat16),
            jax.ShapeDtypeStruct((1, line), jnp.float32),
        ],
        compiler_params=pltpu.CompilerParams(vmem_limit_bytes=LIMIT),
        cost_estimate=pl.CostEstimate(flops=8 * 10**9 * n_src, bytes_accessed=5 * 10**6 * n_src, transcendentals=0),
        name="score",
    )(table[2], here, packed, found, *(array for array, _ in rows), *starts)


def spread_kernel(pair_ref, count_ref, here_ref, packed_ref, weight_ref, *refs, shift, part, sources, picks):
    wide_refs, (far_mem_ref, token_ref, mem_ref, sems) = refs[:sources], refs[-4:]
    token_ref[...] = jnp.zeros(token_ref.shape, jnp.float32)
    final = pl.program_id(0) == pl.num_programs(0) - 1
    slabs = sems.shape[0]
    slab = mem_ref.shape[0] // slabs

    def store(k):
        rows = pl.ds(pl.multiple_of(k * slab, slab), slab)
        far_rows = pl.ds(pl.multiple_of(part * mem_ref.shape[0] + k * slab, slab), slab)
        return pltpu.make_async_copy(mem_ref.at[rows, :], far_mem_ref.at[far_rows, :], sems.at[k])

    def store_upto(had, upto):
        def one(k, _):
            store(k).start()
            return 0

        lax.fori_loop(had, upto, one, 0)
        return jnp.maximum(had, upto)
    each = pl.num_programs(0) // sources
    src = source(picks, here_ref, pl.program_id(0))
    windows = mem_ref.shape[0] // WINDOW

    def window(b):
        return pl.ds(pl.multiple_of(jnp.clip(b - part * windows, 0, windows - 1) * WINDOW, WINDOW), WINDOW)

    @pl.when(pl.program_id(0) == 0)
    def _():
        def clear(b, _):
            mem_ref[pl.ds(pl.multiple_of(b * WINDOW, WINDOW), WINDOW), :] = jnp.zeros((WINDOW, mem_ref.shape[1]), jnp.float32)
            return 0

        lax.fori_loop(0, windows, clear, 0)

    def step(wide_ref, i, had):
        parts = []
        for c, b in pairs_at(pair_ref, src, i, SPREAD_PAIRS):
            c = jnp.where(b == 255, 0, c)
            entry = chunk_of(packed_ref, c) >> shift
            hot = one_hot(entry - b * WINDOW, WINDOW, chunk_of(weight_ref, c))
            parts.append((b, lax.dot_general(hot, wide_ref[0, c], NT, preferred_element_type=jnp.float32)))
        for b, term in parts:
            mem_ref[window(b), :] += term
        most = pair_ref.shape[1] - 1
        ahead = jnp.clip((pair_ref[src, jnp.minimum((i + 1) * SPREAD_PAIRS, most)] & 255) - part * windows, 0, windows)
        return store_upto(had, jnp.where(final & (i + 1 < steps), ahead * WINDOW // slab, 0))

    steps = (count_ref[src] + SPREAD_PAIRS - 1) // SPREAD_PAIRS
    for n, wide_ref in enumerate(wide_refs):

        @pl.when(pl.program_id(0) // each == n)
        def _(wide_ref=wide_ref, n=n):
            had = lax.fori_loop(0, steps, functools.partial(step, wide_ref), 0)
            if n == len(wide_refs) - 1:

                @pl.when(final)
                def _():
                    store_upto(had, slabs)
                    for k in range(slabs):
                        store(k).wait()


def spread(tables, here, picks, packed, weight, wide_rows, entries, shift, part, partly, line, starts):
    n_src, halves, _ = packed.shape
    chunks = halves // HALVES
    width = wide_rows[0].shape[2]
    each = n_src // len(wide_rows)
    pairs, counts = (table[part] for table in tables)
    parts = tables[0].shape[0]
    lists = pl.BlockSpec((1, halves, LANES), lambda s, pairs, counts, here: (source(picks, here, s), 0, 0))
    before = [] if partly is None else [partly]
    return pl.pallas_call(
        functools.partial(spread_kernel, shift=shift, part=part, sources=len(wide_rows), picks=picks),
        grid_spec=pltpu.PrefetchScalarGridSpec(
            num_scalar_prefetch=3,
            grid=(n_src,),
            in_specs=[lists, lists]
            + [
                pl.BlockSpec((1, chunks, width, CHUNK), lambda s, *_, n=n: (jnp.clip(s - n * each, 0, each - 1), 0, 0, 0))
                for n in range(len(wide_rows))
            ]
            + [pl.BlockSpec(memory_space=pl.ANY)] * (len(before) + len(starts)),
            out_specs=[
                pl.BlockSpec(memory_space=pl.ANY),
                pl.BlockSpec((1, line), lambda s, *_: (0, 0)),
            ],
            scratch_shapes=[
                pltpu.VMEM((entries // parts, width), jnp.float32),
                pltpu.SemaphoreType.DMA((slabs_of(entries // parts),)),
            ],
        ),
        out_shape=[
            jax.ShapeDtypeStruct((entries, width), jnp.float32),
            jax.ShapeDtypeStruct((1, line), jnp.float32),
        ],
        input_output_aliases={5 + len(wide_rows): 0} if before else {},
        compiler_params=pltpu.CompilerParams(vmem_limit_bytes=LIMIT),
        cost_estimate=pl.CostEstimate(flops=9 * 10**9 * n_src, bytes_accessed=5 * 10**6 * n_src, transcendentals=0),
        name="spread",
    )(pairs, counts, here, packed, weight, *wide_rows, *before, *starts)


def lists_kernel(ids_ref, place_ref, weight_ref, mine_ref, gain_ref, shift_ref, *refs, shards, parts, owner_rows):
    block_refs, refs = refs[: parts - 1], refs[parts - 1 :]
    packed_ref, scaled_ref, residual_ref, normed_ref, inv_ref, low_ref, got = refs[:7]
    ids, place, weight, out_packed, out_weight = refs[7:12]
    send_packed, recv_packed, send_weight, recv_weight, send_block, recv_block = refs[12:]
    row = lax.axis_index("rows")
    me = lax.axis_index("tp")
    halves = packed_ref.shape[1]
    lines = ids_ref.shape[0]
    requests = lines * LANES
    barrier = pltpu.get_barrier_semaphore()

    def greet(s, _):
        pl.semaphore_signal(barrier, inc=1, device_id={"rows": lax.rem(row + s, shards)}, device_id_type=MESH)
        return 0

    lax.fori_loop(1, shards, greet, 0)
    for s in range(1, parts):
        pl.semaphore_signal(barrier, inc=1, device_id={"tp": lax.rem(me + s, parts)}, device_id_type=MESH)
    block_copies = [
        pltpu.make_async_remote_copy(
            src_ref=block_refs[s - 1], dst_ref=got.at[s - 1], send_sem=send_block.at[s - 1], recv_sem=recv_block.at[s - 1],
            device_id={"tp": lax.rem(me + s, parts)}, device_id_type=MESH,
        )
        for s in range(1, parts)
    ]
    ids[0:lines, :] = ids_ref[...]
    ids[lines:, :] = jnp.full((ids.shape[0] - lines, LANES), -1, jnp.int32)
    place[0:lines, :] = place_ref[...]
    place[lines:, :] = jnp.zeros((ids.shape[0] - lines, LANES), jnp.int32)
    weight[0:lines, :] = weight_ref[...]
    weight[lines:, :] = jnp.zeros((ids.shape[0] - lines, LANES), jnp.float32)

    def prepare(owner):
        below = jnp.sum(jnp.where(ids_ref[...] < owner * owner_rows, 1, 0))
        line = pl.ds((below // CHUNK) * HALVES, halves)
        own = ids[line, :] - owner * owner_rows
        inside = (own >= 0) & (own < owner_rows)
        out_packed[owner] = jnp.where(inside, own * requests + place[line, :], -requests)
        out_weight[owner] = weight[line, :]

    def copies(s):
        owner = lax.rem(row + s, shards)
        return [
            pltpu.make_async_remote_copy(
                src_ref=src.at[owner], dst_ref=dst.at[row], send_sem=send.at[s - 1], recv_sem=recv.at[s - 1],
                device_id={"rows": owner}, device_id_type=MESH,
            )
            for src, dst, send, recv in (
                (out_packed, packed_ref, send_packed, recv_packed),
                (out_weight, scaled_ref, send_weight, recv_weight),
            )
        ]

    prepare(lax.rem(row + 1, shards))
    pl.semaphore_wait(barrier, shards + parts - 2)
    for copy in block_copies:
        copy.start()

    def send(s, _):
        for copy in copies(s):
            copy.start()
        prepare(lax.rem(row + s + 1, shards))
        return 0

    lax.fori_loop(1, shards, send, 0)
    packed_ref[row] = out_packed[row]
    scaled_ref[row] = out_weight[row]

    def finish(s, _):
        for copy in copies(s):
            copy.wait()
        return 0

    for copy in block_copies:
        copy.wait()
    residual = functools.reduce(lambda a, b: a + b, [got[s].astype(jnp.float32) for s in range(parts - 1)], mine_ref[...])
    residual_ref[...] = residual
    residual = residual - jnp.mean(residual, axis=1, keepdims=True)
    inv = lax.rsqrt(jnp.mean(residual * residual, axis=1, keepdims=True) + 1e-05)
    normed = residual * inv
    inv_ref[...] = inv
    normed_ref[...] = normed
    low_ref[...] = (normed * gain_ref[...] + shift_ref[...]).astype(low_ref.dtype)
    lax.fori_loop(1, shards, finish, 0)


def request_lists(memory_ids, score_cotangent, scale, owner_rows, shards, mine, blocks, gain, shift):
    tokens, retrieved = memory_ids.shape
    requests = tokens * retrieved
    capacity = 3 * requests // (2 * shards)
    chunks = -(-(capacity + CHUNK - 1) // CHUNK)
    chains = min(CHAINS, chunks)
    chunks = -(-chunks // chains) * chains

    def line_up(values):
        tiles = values.reshape(retrieved // 8, 8, tokens // LANES, LANES)
        return tiles.transpose(0, 2, 1, 3).reshape(-1)

    flat = line_up(memory_ids.T)
    place = line_up(jnp.arange(requests, dtype=jnp.int32))
    weight = line_up(score_cotangent.T.astype(jnp.float32) * scale)
    ids, place, weight = lax.sort((flat, place, weight), num_keys=1, is_stable=False)
    lines = requests // LANES
    halves = chunks * HALVES
    whole = pl.BlockSpec(memory_space=pltpu.VMEM)
    dma = pltpu.SemaphoreType.DMA
    shape = (shards, halves, LANES)
    rows, full = mine.shape
    return chains, *pl.pallas_call(
        functools.partial(lists_kernel, shards=shards, parts=len(blocks) + 1, owner_rows=owner_rows),
        in_specs=[whole] * 6 + [pl.BlockSpec(memory_space=pltpu.HBM)] * len(blocks),
        out_specs=[whole] * 6,
        out_shape=[
            jax.ShapeDtypeStruct(shape, jnp.int32),
            jax.ShapeDtypeStruct(shape, jnp.float32),
            jax.ShapeDtypeStruct((rows, full), jnp.float32),
            jax.ShapeDtypeStruct((rows, full), jnp.float32),
            jax.ShapeDtypeStruct((rows, 1), jnp.float32),
            jax.ShapeDtypeStruct((rows, full), jnp.bfloat16),
        ],
        scratch_shapes=[
            pltpu.VMEM((len(blocks), rows, full), jnp.bfloat16),
            pltpu.VMEM((lines + halves, LANES), jnp.int32),
            pltpu.VMEM((lines + halves, LANES), jnp.int32),
            pltpu.VMEM((lines + halves, LANES), jnp.float32),
            pltpu.VMEM(shape, jnp.int32),
            pltpu.VMEM(shape, jnp.float32),
        ]
        + [dma((shards - 1,))] * 4
        + [dma((len(blocks),))] * 2,
        compiler_params=pltpu.CompilerParams(collective_id=1, has_side_effects=True, vmem_limit_bytes=LIMIT),
        cost_estimate=pl.CostEstimate(flops=14 * 10**9, bytes_accessed=3 * 10**6, transcendentals=0),
        name="lists",
    )(*(item.reshape(lines, LANES) for item in (ids, place, weight)), mine, gain, shift, *blocks)


def pair_tables(packed, requests, owner_rows, parts, step):
    shards, halves, _ = packed.shape
    chunks = halves // HALVES
    windows = owner_rows // WINDOW
    entry = packed >> log2(requests)
    low = jnp.min(jnp.where(entry >= 0, entry, owner_rows), axis=2).reshape(shards, chunks, HALVES).min(axis=2) // WINDOW
    high = jnp.max(entry, axis=2).reshape(shards, chunks, HALVES).max(axis=2) // WINDOW + 1
    edge = jnp.arange(parts, dtype=jnp.int32)[:, None, None] * (windows // parts)
    low = jnp.maximum(low[None], edge)
    number = jnp.maximum(jnp.minimum(high[None], edge + windows // parts) - low, 0)
    upto = jnp.arange(chunks, dtype=jnp.int32)
    ends = jnp.sum(jnp.where(upto[:, None] <= upto[None, :], number[:, :, :, None], 0), axis=2)
    begins = ends - number
    most = -(-(chunks + windows // parts) // step) * step
    index = jnp.arange(most, dtype=jnp.int32)
    here = (index >= begins[..., None]) & (index < ends[..., None])
    value = upto[:, None] * 256 + (low - begins)[..., None] + index
    idle = (chunks - 1) * 256 + 255
    pairs = idle + jnp.sum(jnp.where(here, value - idle, 0), axis=2)
    used = jnp.max(jnp.where(number > 0, upto + 1, 0), axis=2)
    return pairs, ends[..., -1], used


def finish_kernel(*refs, parts, shards, scores, full_width):
    score_refs, refs = refs[:scores], refs[scores:]
    other_refs, refs = refs[: parts - 1], refs[parts - 1 :]
    stats_ref, norm_ref, small_ref, mine_ref, middle_ref, normed_ref, inv_ref, gain_ref = refs[:8]
    total_ref, score_ref, input_ref, few, got_norm, got_few, vector, got_vector = refs[-14:-6]
    send_norm, recv_norm, send_few, recv_few, send_vector, recv_vector = refs[-6:]
    me = lax.axis_index("tp")
    row = lax.axis_index("rows")
    width = small_ref.shape[1]
    retrieved = score_ref.shape[0]
    barrier = pltpu.get_barrier_semaphore()
    for s in range(1, parts):
        pl.semaphore_signal(barrier, inc=1, device_id={"tp": lax.rem(me + s, parts)}, device_id_type=MESH)

    def greet(s, _):
        pl.semaphore_signal(barrier, inc=1, device_id={"rows": lax.rem(row + s, shards)}, device_id_type=MESH)
        return 0

    lax.fori_loop(1, shards, greet, 0)
    few[0:retrieved, :] = functools.reduce(lambda a, b: a + b, [ref[...] for ref in score_refs])
    few[retrieved:, :] = stats_ref[...]
    vector[0:8, :] = small_ref[...]
    pl.semaphore_wait(barrier, parts + shards - 2)

    def over_tp(s, src, dst, send, recv):
        return pltpu.make_async_remote_copy(
            src_ref=src, dst_ref=dst.at[s - 1], send_sem=send.at[s - 1], recv_sem=recv.at[s - 1],
            device_id={"tp": lax.rem(me + s, parts)}, device_id_type=MESH,
        )

    def columns(q):
        return pl.ds(pl.multiple_of(q * width, 128), width)

    copies = [
        over_tp(s, norm_ref.at[:, columns(lax.rem(me + s, parts))], got_norm, send_norm, recv_norm)
        for s in range(1, parts)
    ]
    few_copies = [over_tp(s, few, got_few, send_few, recv_few) for s in range(1, parts)]
    for copy in copies + few_copies:
        copy.start()
    for copy in copies:
        copy.wait()
    norms = norm_ref[:, columns(me)]
    for s in range(parts - 1):
        norms = norms + got_norm[s]
    vector[8:16, :] = norms

    def to_row(s):
        return pltpu.make_async_remote_copy(
            src_ref=vector, dst_ref=got_vector.at[s - 1], send_sem=send_vector.at[s - 1], recv_sem=recv_vector.at[s - 1],
            device_id={"rows": lax.rem(row + s, shards)}, device_id_type=MESH,
        )

    def send(s, _):
        to_row(s).start()
        return 0

    lax.fori_loop(1, shards, send, 0)
    for copy in few_copies:
        copy.wait()
    few_total = functools.reduce(lambda a, b: a + b, [got_few[s] for s in range(parts - 1)], few[...])
    score_ref[...] = few_total[0:retrieved, :] * (1.0 / math.sqrt(full_width))
    stats = few_total[retrieved:, :] * (1.0 / full_width)
    stats = jnp.concatenate([stats] * (LANES // stats.shape[0]), axis=0).T
    first = functools.reduce(lambda a, b: a + b, [ref[...].astype(jnp.float32) for ref in other_refs], mine_ref[...])
    scaled = first * gain_ref[...]
    input_ref[...] = middle_ref[...] + inv_ref[...] * (scaled - stats[:, 0:1] - normed_ref[...] * stats[:, 1:2])

    def await_row(s, _):
        to_row(s).wait()
        return 0

    lax.fori_loop(1, shards, await_row, 0)
    total_ref[...] = vector[...]

    def add(s, _):
        total_ref[...] += got_vector[s]
        return 0

    lax.fori_loop(0, shards - 1, add, 0)


def finish(scores, others, stats, norms, small, mine, middle, normed, inv, gain, starts, parts, shards):
    width = small.shape[1]
    few = (scores[0].shape[0] + stats.shape[0], stats.shape[1])
    whole = pl.BlockSpec(memory_space=pltpu.VMEM)
    dma = pltpu.SemaphoreType.DMA
    arrays = [*scores, *others, stats, norms, small, mine, middle, normed, inv, gain]
    return pl.pallas_call(
        functools.partial(finish_kernel, parts=parts, shards=shards, scores=len(scores), full_width=norms.shape[1]),
        in_specs=[whole] * len(arrays) + [pl.BlockSpec(memory_space=pl.ANY)] * len(starts),
        out_specs=[whole] * 3,
        out_shape=[
            jax.ShapeDtypeStruct((16, width), jnp.float32),
            jax.ShapeDtypeStruct(scores[0].shape, jnp.float32),
            jax.ShapeDtypeStruct(mine.shape, jnp.float32),
        ],
        scratch_shapes=[
            pltpu.VMEM(few, jnp.float32),
            pltpu.VMEM((parts - 1, 8, width), jnp.float32),
            pltpu.VMEM((parts - 1,) + few, jnp.float32),
            pltpu.VMEM((16, width), jnp.float32),
            pltpu.VMEM((shards - 1, 16, width), jnp.float32),
        ]
        + [dma((parts - 1,))] * 4
        + [dma((shards - 1,))] * 2,
        compiler_params=pltpu.CompilerParams(collective_id=0, has_side_effects=True, vmem_limit_bytes=LIMIT),
        cost_estimate=pl.CostEstimate(flops=16 * 10**9, bytes_accessed=10**6, transcendentals=0),
        name="finish",
    )(*arrays, *starts)


GELU_C = math.sqrt(2.0 / math.pi)
GELU_A = 0.044715


def place_rows(blocks, whole_ref):
    size, own = len(blocks), blocks[0].shape[0]
    me = lax.axis_index("tp")
    for s, block in enumerate(blocks):
        whole_ref[pl.ds(pl.multiple_of(lax.rem(me + size - s, size) * own, own), own), :] = block[...]


def place_columns(blocks, whole_ref):
    size, own = len(blocks), blocks[0].shape[1]
    me = lax.axis_index("tp")
    for s, block in enumerate(blocks):
        whole_ref[:, pl.ds(pl.multiple_of(lax.rem(me + size - s, size) * own, own), own)] = block[...]


def send_rows(whole_ref, own_ref, sends):
    size, own = len(sends) + 1, own_ref.shape[0]
    me = lax.axis_index("tp")

    def rows(s):
        return whole_ref[pl.ds(pl.multiple_of(lax.rem(me + s, size) * own, own), own), :]

    own_ref[...] = rows(0)
    for s, send in enumerate(sends):
        send[...] = rows(s + 1).astype(send.dtype)


def send_columns(whole_ref, own_ref, sends):
    size, own = len(sends) + 1, own_ref.shape[1]
    me = lax.axis_index("tp")

    def columns(s):
        return whole_ref[:, pl.ds(pl.multiple_of(lax.rem(me + s, size) * own, own), own)]

    own_ref[...] = columns(0)
    for s, send in enumerate(sends):
        send[...] = columns(s + 1).astype(send.dtype)


def visible(length_ref, first, rows, keys):
    row = lax.broadcasted_iota(jnp.int32, (rows, 1), 0) + first
    start, bound = jnp.zeros((rows, 1), jnp.int32), 0
    for k in range(length_ref.shape[1]):
        bound = bound + length_ref[0, k]
        start = jnp.where(row >= bound, bound, start)
    key = lax.broadcasted_iota(jnp.int32, (rows, keys), 1)
    return (key <= row) & (key >= start)


def head_lanes(h, width):
    lane = lax.broadcasted_iota(jnp.int32, (1, width), 1)
    return (lane >= h * HD) & (lane < (h + 1) * HD)


def attention_of(query, keys, seen):
    logits = lax.dot_general(query, keys, NT, preferred_element_type=jnp.float32) * (1.0 / math.sqrt(HD))
    logits = jnp.where(seen, logits, -1000000000.0)
    weights = jnp.exp(logits - jnp.max(logits, axis=1, keepdims=True))
    return weights / jnp.sum(weights, axis=1, keepdims=True)


def attend_kernel(length_ref, *refs, parts):
    blocks = refs[:parts]
    gain_ref, shift_ref, w_ref, qv_ref, out_ref, bias_ref = refs[parts : parts + 6]
    outs = refs[parts + 6 :]
    normed_ref, low_ref, inv_ref, qkv_ref, mixed_ref, own_ref = outs[:6]
    sends, (x_ref, part_ref) = outs[6:-2], outs[-2:]
    tokens, width = mixed_ref.shape
    place_columns(blocks, x_ref)
    x = x_ref[...].astype(jnp.float32)
    x = x - jnp.mean(x, axis=1, keepdims=True)
    inv = lax.rsqrt(jnp.mean(x * x, axis=1, keepdims=True) + 1e-05)
    normed = x * inv
    normed_ref[...] = normed
    inv_ref[...] = inv
    low = (normed * gain_ref[...] + shift_ref[...]).astype(jnp.bfloat16)
    low_ref[...] = low
    for c in range(3):
        value = jnp.dot(low, w_ref[c], preferred_element_type=jnp.float32)
        if c != 1:
            value = value + qv_ref[c // 2 : c // 2 + 1, :]
        qkv_ref[c] = value.astype(jnp.bfloat16)
    step = tokens // 2
    for first in (0, step):
        keys = first + step
        seen = visible(length_ref, first, step, keys)
        query = qkv_ref[0, first:keys, :]
        mixed = jnp.zeros((step, width), jnp.float32)
        for h in range(width // HD):
            lanes = head_lanes(h, width)
            attention = attention_of(jnp.where(lanes, query, jnp.zeros_like(query)), qkv_ref[1, :keys, :], seen)
            value = jnp.dot(attention.astype(jnp.bfloat16), qkv_ref[2, :keys, :], preferred_element_type=jnp.float32)
            mixed = jnp.where(lanes, value, mixed)
        mixed_ref[first:keys, :] = mixed.astype(jnp.bfloat16)
    part_ref[...] = jnp.dot(mixed_ref[...], out_ref[...], preferred_element_type=jnp.float32) + bias_ref[...]
    own = own_ref.shape[0]
    mine = pl.ds(pl.multiple_of(lax.axis_index("tp") * own, own), own)
    send_rows(part_ref, own_ref, sends)
    own_ref[...] += x_ref[mine, :].astype(jnp.float32)


def feed_kernel(*refs, parts):
    blocks = refs[:parts]
    residual_ref, up_ref, up_bias_ref, down_ref = refs[parts : parts + 4]
    outs = refs[parts + 4 :]
    low_ref, before_ref, active_ref, own_ref = outs[-5 - parts + 1 : -parts]
    sends, part_ref = outs[-parts:-1], outs[-1]
    place_rows(blocks, low_ref)
    before = jnp.dot(low_ref[...], up_ref[...], preferred_element_type=jnp.float32) + up_bias_ref[...]
    before_ref[...] = before
    bent = jnp.tanh(GELU_C * (before + GELU_A * before * before * before))
    active = (0.5 * before * (1.0 + bent)).astype(jnp.bfloat16)
    active_ref[...] = active
    part_ref[...] = jnp.dot(active, down_ref[...], preferred_element_type=jnp.float32)
    own = residual_ref.shape[0]
    mine = pl.ds(pl.multiple_of(lax.axis_index("tp") * own, own), own)
    part_ref[mine, :] += residual_ref[...]
    send_columns(part_ref, own_ref, sends)


def feed_back_kernel(*refs, parts):
    blocks = refs[:parts]
    low_ref, before_ref, active_ref, up_ref, down_ref = refs[parts : parts + 5]
    outs = refs[-7 - parts :]
    mine_ref, down_grad_ref, up_grad_ref, down_bias_ref, up_bias_ref, own_ref = outs[:6]
    sends, (full_ref, part_ref) = outs[6:-2], outs[-2:]
    place_columns(blocks, full_ref)
    own = mine_ref.shape[0]
    mine = pl.ds(pl.multiple_of(lax.axis_index("tp") * own, own), own)
    mine_ref[...] = full_ref[mine, :]
    down_bias_ref[...] = jnp.broadcast_to(
        jnp.sum(blocks[0][...].astype(jnp.float32), axis=0, keepdims=True), down_bias_ref.shape
    )
    active_grad = lax.dot_general(full_ref[...], down_ref[...], NT, preferred_element_type=jnp.float32)
    before = before_ref[...]
    bent = jnp.tanh(GELU_C * (before + GELU_A * before * before * before))
    slope = 0.5 * (1.0 + bent) + 0.5 * before * (1.0 - bent * bent) * GELU_C * (1.0 + 3.0 * GELU_A * before * before)
    grad = (active_grad * slope).astype(jnp.bfloat16)
    up_bias_ref[...] = jnp.broadcast_to(jnp.sum(grad.astype(jnp.float32), axis=0, keepdims=True), up_bias_ref.shape)
    part_ref[...] = lax.dot_general(grad, up_ref[...], NT, preferred_element_type=jnp.float32)
    send_rows(part_ref, own_ref, sends)
    down_grad_ref[...] = lax.dot_general(
        full_ref[...], active_ref[...], TN, preferred_element_type=jnp.float32
    ).astype(jnp.bfloat16)
    up_grad_ref[...] = lax.dot_general(low_ref[...], grad, TN, preferred_element_type=jnp.float32).astype(jnp.bfloat16)


def attend_back_kernel(length_ref, *refs, parts):
    blocks = refs[:parts]
    out_ref, qkv_ref, mixed_ref, w_ref, low_ref, normed_ref, gain_ref = refs[parts : parts + 7]
    second_gain_ref, second_shift_ref, down_bias_ref, up_bias_ref = refs[parts + 7 : parts + 11]
    outs = refs[-10 - parts :]
    middle_ref, normed_own_ref, gain_own_ref, weight_grad_ref, stats_ref, norm_ref, small_ref, own_ref = outs[:8]
    sends = outs[8 : 7 + parts]
    full_ref, part_ref, stacked_ref = outs[-3:]
    tokens, width = mixed_ref.shape
    place_rows(blocks, full_ref)
    columns = pl.ds(pl.multiple_of(lax.axis_index("tp") * width, width), width)
    middle_ref[...] = full_ref[:, columns].astype(jnp.float32)
    normed_own_ref[...] = normed_ref[:, columns]
    gain_own_ref[...] = gain_ref[:, columns]
    grad = lax.dot_general(full_ref[...], out_ref[...], NT, preferred_element_type=jnp.float32).astype(jnp.bfloat16)
    step = tokens // 2
    stacked_ref[...] = jnp.zeros(stacked_ref.shape, jnp.float32)
    scale = 1.0 / math.sqrt(HD)
    for first in (0, step):
        keys = first + step
        seen = visible(length_ref, first, step, keys)
        query = qkv_ref[0, first:keys, :]
        out_grad = grad[first:keys, :]
        key, value = qkv_ref[1, :keys, :], qkv_ref[2, :keys, :]
        for h in range(width // HD):
            lanes = head_lanes(h, width)
            query_h = jnp.where(lanes, query, jnp.zeros_like(query))
            grad_h = jnp.where(lanes, out_grad, jnp.zeros_like(out_grad))
            attention = attention_of(query_h, key, seen)
            attention_grad = lax.dot_general(grad_h, value, NT, preferred_element_type=jnp.float32)
            delta = jnp.sum(attention * attention_grad, axis=1, keepdims=True)
            logit_grad = (attention * (attention_grad - delta)).astype(jnp.bfloat16)
            query_grad = jnp.dot(logit_grad, key, preferred_element_type=jnp.float32) * scale
            stacked_ref[0, first:keys, :] += jnp.where(lanes, query_grad, 0.0)
            stacked_ref[1, :keys, :] += lax.dot_general(logit_grad, query_h, TN, preferred_element_type=jnp.float32) * scale
            stacked_ref[2, :keys, :] += lax.dot_general(
                attention.astype(jnp.bfloat16), grad_h, TN, preferred_element_type=jnp.float32
            )
    first_part = jnp.zeros(part_ref.shape, jnp.float32)
    small = []
    for c in range(3):
        item = stacked_ref[c].astype(jnp.bfloat16)
        small.append(jnp.sum(item.astype(jnp.float32), axis=0, keepdims=True))
        weight_grad_ref[:, c * width : (c + 1) * width] = lax.dot_general(
            low_ref[...], item, TN, preferred_element_type=jnp.float32
        ).astype(jnp.bfloat16)
        first_part += lax.dot_general(item, w_ref[c], NT, preferred_element_type=jnp.float32)
    part_ref[...] = first_part
    send_columns(part_ref, own_ref, sends)
    small_ref[...] = jnp.concatenate(
        [small[0], small[2], jnp.sum(middle_ref[...], axis=0, keepdims=True), down_bias_ref[0:1, :]]
        + [up_bias_ref[0:1, k * width : (k + 1) * width] for k in range(parts)],
        axis=0,
    )
    normed = normed_ref[...]
    norm_ref[...] = jnp.concatenate(
        [
            second_gain_ref[...],
            second_shift_ref[...],
            jnp.sum(first_part * normed, axis=0, keepdims=True),
            jnp.sum(first_part, axis=0, keepdims=True),
            jnp.zeros((4, first_part.shape[1]), jnp.float32),
        ],
        axis=0,
    )
    scaled = first_part * gain_ref[...]
    lane = lax.broadcasted_iota(jnp.int32, (1, LANES), 1)
    stats = jnp.where(lane == 0, jnp.sum(scaled, axis=1, keepdims=True), 0.0) + jnp.where(
        lane == 1, jnp.sum(scaled * normed, axis=1, keepdims=True), 0.0
    )
    stats_ref[...] = stats.T[0:8, :]
    weight_grad_ref[:, 3 * width :] = lax.dot_general(
        full_ref[...], mixed_ref[...], TN, preferred_element_type=jnp.float32
    ).astype(jnp.bfloat16)


def unpack_kernel(attend_ref, up_ref, down_ref, qkv_grad_ref, out_grad_ref, up_grad_ref, down_grad_ref, *, parts):
    width = out_grad_ref.shape[0]
    for c in range(3):
        qkv_grad_ref[c] = attend_ref[:, c * width : (c + 1) * width].astype(jnp.float32)
    out_grad_ref[...] = attend_ref[:, 3 * width :].astype(jnp.float32).T
    up_grad_ref[...] = up_ref[...].astype(jnp.float32)
    down_grad_ref[...] = down_ref[...].astype(jnp.float32).T


def block_call(name, kernel, lengths, arrays, starts, outs, scratch, flops, parts):
    whole = pl.BlockSpec(memory_space=pltpu.VMEM)
    scalars = [] if lengths is None else [lengths]
    return pl.pallas_call(
        functools.partial(kernel, parts=parts),
        in_specs=[pl.BlockSpec(memory_space=pltpu.SMEM)] * len(scalars)
        + [whole] * len(arrays)
        + [pl.BlockSpec(memory_space=pl.ANY)] * len(starts),
        out_specs=[whole] * len(outs),
        out_shape=[jax.ShapeDtypeStruct(shape, dtype) for shape, dtype in outs],
        scratch_shapes=[pltpu.VMEM(shape, dtype) for shape, dtype in scratch],
        compiler_params=pltpu.CompilerParams(vmem_limit_bytes=LIMIT),
        cost_estimate=pl.CostEstimate(flops=flops, bytes_accessed=10**7, transcendentals=0),
        name=name,
    )(*scalars, *arrays, *starts)


def permute(value, axis, step):
    size = lax.axis_size(axis)
    return lax.ppermute(value, axis, [(i, (i + step) % size) for i in range(size)])


def exchange(block_for, axis, stride=1):
    size = lax.axis_size(axis)
    me = lax.axis_index(axis)
    return [permute(block_for(lax.rem(me + s, size)), axis, s) for s in range(stride, size, stride)]


def deliver(sends):
    return [permute(block, "tp", s + 1) for s, block in enumerate(sends)]


def spread_out(value):
    return [value] + exchange(lambda q: value, "tp")


def total(mine, others, zero=None):
    first = mine.astype(jnp.float32)
    if zero is not None:
        first = first + zero[:, : mine.shape[-1]]
    return functools.reduce(lambda a, b: a + b.astype(jnp.float32), others, first)


def scatter_rows(value):
    return lax.psum_scatter(value, "rows", scatter_dimension=0, tiled=True)


def pair_swap(value):
    size = lax.axis_size("rows")
    return lax.ppermute(value, "rows", [(i, i ^ 1) for i in range(size)])


def on_device(
    block_input,
    first_gain,
    first_shift,
    qkv_weight,
    qv_bias,
    out_weight,
    out_bias,
    second_gain,
    second_shift,
    up_weight,
    up_bias,
    down_weight,
    down_bias,
    memory_keys,
    memory_ids,
    doc_lengths,
    out_cotangent,
    score_cotangent,
):
    row_count, width = block_input.shape
    full_width = out_weight.shape[1]
    shards = lax.axis_size("rows")
    parts = lax.axis_size("tp")
    retrieved = memory_ids.shape[1]
    owner_rows = memory_keys.shape[0]
    part = lax.axis_index("tp")
    offset = part * width
    own_tokens = row_count // parts
    memory_scale = 1.0 / math.sqrt(full_width)

    inputs = spread_out(block_input)

    f32, bf16 = jnp.float32, jnp.bfloat16
    bias_wide = lax.dynamic_update_slice_in_dim(jnp.zeros((1, full_width), f32), out_bias[None], offset, 1)
    normed_first, first_low, inv_first, qkv_low, mixed_heads, mine, *sends = block_call(
        "attend",
        attend_kernel,
        doc_lengths,
        [*inputs, first_gain[None], first_shift[None], qkv_weight, qv_bias, out_weight, bias_wide],
        [],
        [
            ((row_count, full_width), f32),
            ((row_count, full_width), bf16),
            ((row_count, 1), f32),
            ((3, row_count, width), bf16),
            ((row_count, width), bf16),
            ((own_tokens, full_width), f32),
        ]
        + [((own_tokens, full_width), bf16)] * (parts - 1),
        [((row_count, full_width), bf16), ((row_count, full_width), f32)],
        9 * 10**9,
        parts,
    )

    chains, packed, weight, residual_mid, normed_second, inv_second, second_own = request_lists(
        memory_ids,
        score_cotangent,
        memory_scale,
        owner_rows,
        shards,
        mine,
        sends,
        second_gain[None],
        second_shift[None],
    )
    requests = row_count * retrieved
    shift = log2(requests)
    table = tuple(item[0] for item in pair_tables(packed, requests, owner_rows, 1, PAIRS))
    pieces = PARTS if owner_rows // WINDOW % PARTS == 0 else 1
    tables = pair_tables(packed, requests, owner_rows, pieces, SPREAD_PAIRS)[:2]
    direct = shards == 2 * CHIPS
    here = lax.axis_index("rows").astype(jnp.int32)[None]
    near, far = ([(away, other) for away in (1, 2, 3, 0)] for other in (False, True))
    if direct:
        orders = [far[:2] + near[:2], far[2:], near[2:]]
        score_orders = [near[:2], near[2:], far[:2], far[2:]]
    else:
        orders = score_orders = [None]
    found, grads, zeros = [], [], []

    def fetch_next(*starts):
        n = len(found)
        if n < len(orders):
            found_part, grad_part, token = fetch(
                table, here, orders[n], packed, weight, memory_keys, row_count, retrieved, chains, full_width, starts
            )
            found.append(found_part)
            grads.append(grad_part)
            zeros.append(token)
        return zeros[-1]

    seconds = spread_out(second_own)
    fetch_next(second_own)
    second_low, before, active, mine, *sends = block_call(
        "feed",
        feed_kernel,
        None,
        [*seconds, residual_mid, up_weight, up_bias[None], down_weight],
        [grads[-1]],
        [
            ((row_count, full_width), bf16),
            ((row_count, up_bias.shape[0]), f32),
            ((row_count, up_bias.shape[0]), bf16),
            ((row_count, width), f32),
        ]
        + [((row_count, width), bf16)] * (parts - 1),
        [((row_count, full_width), f32)],
        8 * 10**9,
        parts,
    )
    others = deliver(sends)
    if direct:
        twin = pair_swap(grads[0][:2])
        summed = [total(grads[0][2 + n], [twin[n]]).astype(bf16) for n in (0, 1)]
        moved = [permute(summed[n], "rows", 2 * (n + 1)) for n in (0, 1)]
    zero = fetch_next(mine, *(summed if direct else ()))
    output_low = (total(mine, others, zero) + down_bias).astype(jnp.bfloat16)
    if direct:
        twin = pair_swap(grads[1])
        rows_near = exchange(lambda q: output_low, "rows", 2)[::-1]
        zero = fetch_next(output_low)
        rows_near = [row[None] for row in rows_near] + [output_low[None]]
        rows_far = pair_swap(jnp.concatenate(rows_near))
        score_rows = [
            [(rows_near[0], 0), (rows_near[1], 0)],
            [(rows_near[2], 0), (rows_near[3], 0)],
            [(rows_far, 0), (rows_far, 1)],
            [(rows_far, 2), (rows_far, 3)],
        ]
        moved.append(permute(total(grads[2][0], [twin[0]], zero).astype(bf16), "rows", 6))
        mine = total(grads[2][1], [twin[1]])
        score_found = [(found[0], 1), (found[2], 0), (found[0], 0), (found[1], 0)]
    else:
        memory_part = lax.psum_scatter(grads[0].reshape(-1, width), "rows", scatter_dimension=0, tiled=True)
        score_rows = [[(lax.all_gather(output_low, "rows", axis=0, tiled=False), None)]]
        score_found = [(found[0], 0)]
    score_parts, wide_rows = [], []

    def score_next(*starts):
        n = len(score_parts)
        if n < len(score_orders):
            score_part, wide_part, token = score(
                table, here, score_orders[n], packed, *score_found[n], score_rows[n], retrieved, chains, full_width, starts
            )
            score_parts.append(score_part)
            wide_rows.append(wide_part)
            zeros.append(token)
        return zeros[-1]

    zero = score_next(grads[-1])
    if direct:
        memory_part = total(mine, moved, zero)
    grad_out = out_cotangent.astype(jnp.float32) + memory_part
    down_low = grad_out.astype(jnp.bfloat16)
    downs = spread_out(down_low)
    score_next(down_low)
    down_mine, down_weight_low, up_weight_low, down_bias_grad, up_bias_grad, mine, *sends = block_call(
        "feed_back",
        feed_back_kernel,
        None,
        [*downs, second_low, before, active, up_weight, down_weight],
        [wide_rows[-1]],
        [
            ((own_tokens, full_width), bf16),
            ((full_width, up_bias.shape[0]), bf16),
            ((full_width, up_bias.shape[0]), bf16),
            ((8, width), f32),
            ((8, up_bias.shape[0]), f32),
            ((own_tokens, full_width), f32),
        ]
        + [((own_tokens, full_width), bf16)] * (parts - 1),
        [((row_count, full_width), bf16), ((row_count, full_width), f32)],
        14 * 10**9,
        parts,
    )
    others = deliver(sends)
    down_weight_grad = scatter_rows(down_weight_low)
    up_weight_grad = scatter_rows(up_weight_low)
    if direct:
        score_next(mine, down_weight_low, up_weight_low)
    second_grad = total(mine, others, zeros[-1])
    scaled = second_grad * second_gain
    row_first = jnp.mean(scaled, axis=1, keepdims=True)
    row_second = jnp.mean(scaled * normed_second, axis=1, keepdims=True)
    mid_own = down_mine.astype(jnp.float32) + inv_second * (scaled - row_first - normed_second * row_second)
    second_norm_grads = [jnp.sum(item, axis=0, keepdims=True) for item in (second_grad * normed_second, second_grad)]
    mid_low = mid_own.astype(jnp.bfloat16)
    order = sum(score_orders, []) if direct else None
    partly = []

    def spread_next(*starts):
        n = len(partly)
        if n < pieces:
            mem, token = spread(
                tables, here, order, packed, weight, wide_rows, owner_rows, shift, n, partly[-1] if n else None, full_width, starts
            )
            partly.append(mem)
            zeros.append(token)
        return zeros[-1]

    middles = spread_out(mid_low)
    if direct:
        score_next(mid_low)
        score_twin = [pair_swap(score_part) for score_part in score_parts[2:]]
        score_sum = [total(score_parts[0], score_twin[:1], zeros[-1][:, :row_count])]
    mid_columns, normed_own, gain_own, attend_low, row_parts, norm_parts, small, mine, *sends = block_call(
        "attend_back",
        attend_back_kernel,
        doc_lengths,
        [*middles, out_weight, qkv_low, mixed_heads, qkv_weight, first_low, normed_first, first_gain[None]]
        + [*second_norm_grads, down_bias_grad, up_bias_grad],
        [score_sum[0], down_weight_grad] if direct else [],
        [
            ((row_count, width), f32),
            ((row_count, width), f32),
            ((1, width), f32),
            ((full_width, 4 * width), bf16),
            ((8, row_count), f32),
            ((8, full_width), f32),
            ((8, width), f32),
            ((row_count, width), f32),
        ]
        + [((row_count, width), bf16)] * (parts - 1),
        [((row_count, full_width), bf16), ((row_count, full_width), f32), ((3, row_count, width), f32)],
        14 * 10**9,
        parts,
    )
    others = deliver(sends)
    if direct:
        score_sum.append(total(score_parts[1], score_twin[1:], row_parts[2:3]))
        score_moved = [permute(score_sum[n // 2][n % 2], "rows", 2 * (n + 1)) for n in range(3)]
    attend_grad = scatter_rows(attend_low)
    if direct:
        scores = [score_sum[1][1], *score_moved]
    else:
        scores = [lax.psum_scatter(score_parts[0].reshape(-1, row_count), "rows", scatter_dimension=0, tiled=True)]
    zero = spread_next(mine, *([*score_moved[:2], score_sum[1]] if direct else []))
    totals, memory_scores, input_grad = finish(
        scores,
        others,
        row_parts,
        norm_parts,
        small,
        mine,
        mid_columns,
        normed_own,
        inv_first,
        gain_own,
        [zero],
        parts,
        shards,
    )
    own_rows, up_width = up_weight_grad.shape
    qkv_grad, out_weight_grad, up_weight_grad, down_weight_grad = block_call(
        "unpack",
        unpack_kernel,
        None,
        [attend_grad, up_weight_grad, down_weight_grad],
        [],
        [((3, own_rows, width), f32), ((width, own_rows), f32), ((own_rows, up_width), f32), ((up_width, own_rows), f32)],
        [],
        3 * 10**9,
        parts,
    )
    return (
        output_low,
        memory_scores.T,
        input_grad,
        totals[10],
        totals[11],
        qkv_grad,
        totals[0:2],
        out_weight_grad,
        totals[2],
        totals[8],
        totals[9],
        up_weight_grad,
        totals[4:8].reshape(-1),
        down_weight_grad,
        totals[3],
        partly[-1],
    )


def solution(mesh):
    return jax.shard_map(
        on_device,
        mesh=mesh,
        in_specs=(
            P("rows", "tp"),
            P(),
            P(),
            P(None, None, "tp"),
            P(None, "tp"),
            P("tp", None),
            P("tp"),
            P(),
            P(),
            P(None, "tp"),
            P("tp"),
            P("tp", None),
            P("tp"),
            P("rows", "tp"),
            P("rows", None),
            P("rows", None),
            P("rows", "tp"),
            P("rows", None),
        ),
        out_specs=(
            P("rows", "tp"),
            P("rows", None),
            P("rows", "tp"),
            P("tp"),
            P("tp"),
            P(None, "rows", "tp"),
            P(None, "tp"),
            P("tp", "rows"),
            P("tp"),
            P("tp"),
            P("tp"),
            P("rows", "tp"),
            P("tp"),
            P("tp", "rows"),
            P("tp"),
            P("rows", "tp"),
        ),
        check_vma=False,
    )
```
